512 devices in a mesh: ctx: 64 (over z_hi, x, y), tp: 8 (over z_lo, core).
Axes of the slice: x: 4, y: 4, z: 16 (z_hi: 4, z_lo: 4; z = z_hi * 4 + z_lo), core: 2. Of those that a mesh axis runs over, the one named last changes fastest.
Arguments:
- queries: bfloat16 [32768, 8192], P(('ctx', 'tp')), may hold values from -150 to 150
- keys: bfloat16 [32768, 1024], P(('ctx', 'tp')), may hold values from -8 to 8
- values: bfloat16 [32768, 1024], P(('ctx', 'tp')), may hold values from -6 to 6
- out_grad: bfloat16 [32768, 8192], P(('ctx', 'tp')), may hold values from -6 to 6
- ancestors: int32 [128, 2], P('ctx'), may hold values from 0 to 127, as said below
- depths: int32 [128], P('ctx'), may hold values from 0 to 2
- lengths: int32 [128], replicated, may hold values from 128 to 256, as said below
Outputs:
- attended: bfloat16 [32768, 8192], P(('ctx', 'tp'))
- query_grad: bfloat16 [32768, 8192], P(('ctx', 'tp'))
- key_grad: bfloat16 [32768, 1024], P(('ctx', 'tp'))
- value_grad: bfloat16 [32768, 1024], P(('ctx', 'tp'))
The draws below stay inside these ranges and needn't reach their ends.
Inputs may be any that keep to these rules, and one draw needn't show every extreme that they name: Row b holds the ancestors of block b root first in its first depths[b] entries, each smaller than b; the list of each ancestor is a prefix of b's; every ancestor lies on the ctx index of b (block a lies on index a // 2) or on one of the 3 indices before it; the other entries equal b. The last block has 2 ancestors. `lengths`: valid slots of a block come first.
All inputs are finite; a program needn't handle non-finite values.
Results may differ from the reference program's by a relative error of at most 0.03.
Values may be sent and summed in bfloat16 or wider, within the bound.
No kernel may reach another device: no remote copies, remote signals or barrier semaphores. Data moves between devices by JAX's collectives and lax.ppermute only.
A program may use at most 64 MiB of HBM per device.

```python
import jax
import jax.numpy as jnp
from jax import lax

HEADS = 64
KV_HEADS = 8
HEAD_DIM = 128
GROUP = 8
BLK = 256
BLOCKS_DEV = 2
ANC = 2
W = 4
NBLK = 128
TOKENS = 32768


def tree_tables(key):
    key = jax.random.fold_in(key, 11)
    rand_par = jax.random.randint(jax.random.fold_in(key, 1), (NBLK,), 0, 1 << 20, dtype=jnp.int32)
    rand_root = jax.random.randint(jax.random.fold_in(key, 2), (NBLK,), 0, 6, dtype=jnp.int32)
    columns = jnp.arange(ANC, dtype=jnp.int32)
    anc = jnp.broadcast_to(jnp.arange(NBLK, dtype=jnp.int32)[:, None], (NBLK, ANC))
    counts = jnp.zeros((NBLK,), jnp.int32)
    roots = jnp.arange(NBLK, dtype=jnp.int32)

    def visit(block, state):
        anc, counts, roots = state
        lower = jnp.maximum((block // BLOCKS_DEV - (W - 1)) * BLOCKS_DEV, 0)
        span = block - lower
        forced = (block >= 1) & (block <= ANC)
        pick = lower + rand_par[block] % jnp.maximum(span, 1)
        pick = jnp.where(forced, block - 1, pick)
        pick = jnp.where(counts[pick] == ANC, anc[pick, ANC - 1], pick)
        keep = (span > 0) & ((rand_root[block] != 0) | forced) & (roots[pick] >= lower)
        tail = block - (NBLK - W)
        in_tail = tail >= 0
        pick = jnp.where(in_tail & (tail <= 2), NBLK - W, jnp.where(in_tail, block - 1, pick))
        keep = jnp.where(in_tail, tail >= 1, keep)
        depth_p = counts[pick]
        row = jnp.where(columns < depth_p, anc[pick], block)
        row = jnp.where(columns == depth_p, pick, row)
        row = jnp.where(keep, row, block)
        anc = anc.at[block].set(row)
        counts = counts.at[block].set(jnp.where(keep, depth_p + 1, 0))
        roots = roots.at[block].set(jnp.where(keep, roots[pick], block))
        return (anc, counts, roots)
    anc, counts, roots = lax.fori_loop(0, NBLK, visit, (anc, counts, roots))
    return (anc, counts)


def key_base(key):
    return jax.random.truncated_normal(jax.random.fold_in(key, 21), -6.0, 6.0, (TOKENS, KV_HEADS * HEAD_DIM), jnp.float32)


def draw_ancestors(key, part):
    tables = tree_tables(key)
    return tables[0]


def draw_depths(key, part):
    tables = tree_tables(key)
    return tables[1]


def draw_lengths(key, part):
    key = jax.random.fold_in(key, 7)
    sizes = jax.random.randint(key, (NBLK,), BLK // 2, BLK + 1, dtype=jnp.int32)
    return sizes.at[0].set(BLK)


def draw_keys(key, part):
    base = key_base(key)
    return base.astype(jnp.bfloat16)


def draw_queries(key, part):
    key = jax.random.fold_in(key, 5)
    drawn = jax.random.truncated_normal(key, -6.0, 6.0, (TOKENS, HEADS * HEAD_DIM), jnp.float32)
    return drawn.astype(jnp.bfloat16)


def block_levels(own_key, shape, split, low, top_value):
    gain = 1.0
    for dim, shards_of in split:
        draws = jax.random.uniform(jax.random.fold_in(jax.random.fold_in(own_key, 6), dim), (shards_of,), jnp.float32, low / len(split), top_value / len(split))
        gain = gain * jnp.repeat(jnp.exp(draws), shape[dim] // shards_of).reshape((-1,) + (1,) * (len(shape) - 1 - dim))
    return gain


def centred(rng, dims, deviation, limit, cuts=(), held_as=jnp.bfloat16):
    array = deviation * jax.random.normal(rng, dims, jnp.float32)
    if cuts:
        array = array * block_levels(rng, dims, cuts, -0.22, 0.18)
    return jnp.clip(array, -limit, limit).astype(held_as)


def setup_inputs(seed: int = 0) -> dict:
    splits = jax.random.split(jax.random.key(seed), 8)
    return {
        "queries": draw_queries(jax.random.fold_in(splits[7], 71), 0),
        "keys": draw_keys(jax.random.fold_in(splits[7], 71), 0),
        "values": centred(splits[2], (TOKENS, KV_HEADS * HEAD_DIM), 1.0, 6.0, ((0, 512),)),
        "out_grad": centred(splits[3], (TOKENS, HEADS * HEAD_DIM), 1.0, 6.0, ((0, 512),)),
        "ancestors": draw_ancestors(jax.random.fold_in(splits[7], 71), 0),
        "depths": draw_depths(jax.random.fold_in(splits[7], 71), 0),
        "lengths": draw_lengths(jax.random.fold_in(splits[7], 71), 0),
    }


def block_pass(q_blk, g_blk, k_keys, v_keys, slot_ok, key_len, own_len):
    slots = ANC + 1
    positions = jnp.arange(BLK, dtype=jnp.int32)
    slot_ids = jnp.arange(slots, dtype=jnp.int32)
    key_mask = slot_ok[:, None] & (positions[None, :] < key_len[:, None])
    causal = (slot_ids[None, :, None] < ANC) | (positions[None, None, :] <= positions[:, None, None])
    allowed = (key_mask[None, :, :] & causal).reshape(BLK, slots * BLK)
    scale = HEAD_DIM ** -0.5
    qf = q_blk.astype(jnp.float32)
    kf = k_keys.astype(jnp.float32)
    vf = v_keys.astype(jnp.float32)
    scores = jnp.einsum('qhgd,khd->hgqk', qf, kf) * scale
    scores = jnp.where(allowed[None, None], scores, jnp.float32(-1e30))
    top = jnp.max(scores, axis=-1, keepdims=True)
    expo = jnp.exp(scores - top)
    prob = expo / jnp.sum(expo, axis=-1, keepdims=True)
    prob_b = prob.astype(jnp.bfloat16)
    attn = jnp.einsum('hgqk,khd->qhgd', prob_b.astype(jnp.float32), vf)
    q_valid = (positions < own_len)[:, None, None, None]
    attended = jnp.where(q_valid, attn, jnp.float32(0.0)).astype(jnp.bfloat16)
    grad_m = jnp.where(q_valid, g_blk, jnp.zeros_like(g_blk))
    gf = grad_m.astype(jnp.float32)
    delta = jnp.sum(gf * attended.astype(jnp.float32), axis=-1)
    delta = jnp.transpose(delta, (1, 2, 0))
    dprob = jnp.einsum('qhgd,khd->hgqk', gf, vf)
    dscore = (prob * (dprob - delta[..., None])).astype(jnp.bfloat16)
    dsf = dscore.astype(jnp.float32)
    q_grad = (jnp.einsum('hgqk,khd->qhgd', dsf, kf) * scale).astype(jnp.bfloat16)
    k_part = jnp.einsum('hgqk,qhgd->khd', dsf, qf) * scale
    v_part = jnp.einsum('hgqk,qhgd->khd', prob_b.astype(jnp.float32), gf)
    return attended, q_grad, k_part, v_part


def reference(queries, keys, values, out_grad, ancestors, depths, lengths):
    slots = ANC + 1
    q_all = queries.reshape(NBLK, BLK, KV_HEADS, GROUP, HEAD_DIM)
    g_all = out_grad.reshape(NBLK, BLK, KV_HEADS, GROUP, HEAD_DIM)
    k_all = keys.reshape(NBLK, BLK, KV_HEADS, HEAD_DIM)
    v_all = values.reshape(NBLK, BLK, KV_HEADS, HEAD_DIM)

    def visit(carry, block):
        k_acc, v_acc = carry
        ids = jnp.concatenate([ancestors[block], block[None]]).astype(jnp.int32)
        slot_ok = jnp.concatenate([jnp.arange(ANC, dtype=jnp.int32) < depths[block], jnp.ones((1,), dtype=jnp.bool_)])
        k_keys = k_all[ids].reshape(slots * BLK, KV_HEADS, HEAD_DIM)
        v_keys = v_all[ids].reshape(slots * BLK, KV_HEADS, HEAD_DIM)
        attended, q_grad, k_part, v_part = block_pass(q_all[block], g_all[block], k_keys, v_keys, slot_ok, lengths[ids], lengths[block])
        k_acc = k_acc.at[ids].add(k_part.reshape(slots, BLK, KV_HEADS, HEAD_DIM))
        v_acc = v_acc.at[ids].add(v_part.reshape(slots, BLK, KV_HEADS, HEAD_DIM))
        return (k_acc, v_acc), (attended, q_grad)

    zeros = jnp.zeros((NBLK, BLK, KV_HEADS, HEAD_DIM), jnp.float32)
    (k_acc, v_acc), (attended, q_grad) = lax.scan(visit, (zeros, zeros), jnp.arange(NBLK, dtype=jnp.int32))
    wide = HEADS * HEAD_DIM
    narrow = KV_HEADS * HEAD_DIM
    return (attended.reshape(TOKENS, wide), q_grad.reshape(TOKENS, wide),
            k_acc.astype(jnp.bfloat16).reshape(TOKENS, narrow), v_acc.astype(jnp.bfloat16).reshape(TOKENS, narrow))
```

```python
import functools

import jax
import jax.numpy as jnp
from jax import lax
from jax.experimental import pallas as pl
from jax.experimental.pallas import tpu as pltpu
from jax.sharding import Mesh
from jax.sharding import PartitionSpec as P

HEAD_DIM = 128
BLK = 256
ANC = 2
W = 4
QUART = 4
GROUP = 8
PAIR = 2
ROWS = BLK // QUART
WIDE = PAIR * GROUP * HEAD_DIM
NARROW = PAIR * HEAD_DIM
PACK = 2 * WIDE + 2 * NARROW
PLANE = 16
BLOCKS = 2
PREV = (W - 1) * BLOCKS
OWN = PLANE * BLOCKS
RELAYS = PLANE * BLOCKS
PIECE = BLK // 8
KEYS = ANC * BLK + BLK
STEP = 2
NEG = -1e30
LOG2E = 1.4426950408889634
SCALE = HEAD_DIM ** (-0.5)
VMEM = 48 * 1024 * 1024


def whole(count):
    return [pl.BlockSpec(memory_space=pltpu.VMEM)] * count


def smem():
    return pl.BlockSpec(memory_space=pltpu.SMEM)


def gather_kernel(idx_ref, prev_ref, own_ref, out_ref, table):
    table[0:PREV] = prev_ref[...]
    table[PREV:] = own_ref[...]
    for entry in range(RELAYS * ANC):
        out_ref[entry] = table[idx_ref[entry]]


def gather_pieces(idx, prev, own):
    return pl.pallas_call(
        gather_kernel,
        out_shape=jax.ShapeDtypeStruct((RELAYS * ANC, PIECE, HEAD_DIM), jnp.bfloat16),
        in_specs=[smem()] + whole(2),
        out_specs=whole(1)[0],
        scratch_shapes=[pltpu.VMEM((PREV + OWN, PIECE, HEAD_DIM), jnp.bfloat16)],
        compiler_params=pltpu.CompilerParams(vmem_limit_bytes=VMEM),
    )(idx, prev, own)


def scatter_kernel(idx_ref, terms_ref, prev_ref, own_ref, table):
    table[...] = jnp.zeros_like(table)
    for entry in range(RELAYS * ANC):
        place = idx_ref[entry]
        table[place] = table[place] + terms_ref[entry].astype(jnp.float32)
    prev_ref[...] = table[0:PREV].astype(jnp.bfloat16)
    own_ref[...] = table[PREV:]


def scatter_pieces(idx, terms):
    return pl.pallas_call(
        scatter_kernel,
        out_shape=(
            jax.ShapeDtypeStruct((PREV, PIECE, HEAD_DIM), jnp.bfloat16),
            jax.ShapeDtypeStruct((OWN, PIECE, HEAD_DIM), jnp.float32),
        ),
        in_specs=[smem()] + whole(1),
        out_specs=tuple(whole(2)),
        scratch_shapes=[pltpu.VMEM((PREV + OWN, PIECE, HEAD_DIM), jnp.float32)],
        compiler_params=pltpu.CompilerParams(vmem_limit_bytes=VMEM),
    )(idx, terms)


def dot(a, b, dims):
    return lax.dot_general(a, b, (dims, ((), ())), preferred_element_type=jnp.float32)


def attention_kernel(
    info_ref, in0, in1, in2, in3, anc_ref, out0, out1, out2, out3, danc_ref,
    keys, vals, keys_t, vals_t, bias, k_acc, v_acc,
):
    ins = (in0, in1, in2, in3)
    outs = (out0, out1, out2, out3)
    me = info_ref[0]
    own_len = info_ref[1]

    def own_pos(shape, dim):
        row = lax.broadcasted_iota(jnp.int32, shape, dim)
        return ((row // ROWS) ^ me) * ROWS + row % ROWS

    row = lax.broadcasted_iota(jnp.int32, (ANC * BLK, BLK), 0)
    slot = (row // PIECE) % ANC
    place = ((row // 8) % QUART) * ROWS + (row // (ANC * PIECE)) * 8 + row % 8
    limit = jnp.where(slot == 0, info_ref[2], info_ref[3])
    bias[0 : ANC * BLK] = jnp.where(place < limit, jnp.float32(0.0), jnp.float32(NEG))
    key_pos = own_pos((BLK, BLK), 0)
    query_pos = own_pos((BLK, BLK), 1)
    bias[ANC * BLK :] = jnp.where(
        (key_pos <= query_pos) & (key_pos < own_len), jnp.float32(0.0), jnp.float32(NEG)
    )
    live = own_pos((1, BLK), 1) < own_len

    for head in range(PAIR):
        col = 2 * WIDE + head * HEAD_DIM
        keys[head, 0 : ANC * BLK] = anc_ref[head]
        vals[head, 0 : ANC * BLK] = anc_ref[PAIR + head]
        for x in range(QUART):
            at = ANC * BLK + x * ROWS
            keys[head, at : at + ROWS] = ins[x][:, col : col + HEAD_DIM]
            vals[head, at : at + ROWS] = ins[x][:, col + NARROW : col + NARROW + HEAD_DIM]
        keys_t[head] = keys[head].T
        vals_t[head] = vals[head].T
    k_acc[...] = jnp.zeros_like(k_acc)
    v_acc[...] = jnp.zeros_like(v_acc)

    def one(head, q, g):
        k, v = keys[head], vals[head]
        s = dot(k, q, ((1,), (1,))) + bias[...]
        dp = dot(v, g, ((1,), (1,)))
        top = jnp.max(s, axis=0, keepdims=True)
        e = jnp.exp2((s - top) * jnp.float32(SCALE * LOG2E))
        total = jnp.sum(e, axis=0, keepdims=True)
        mixed = jnp.sum(e * dp, axis=0, keepdims=True)
        inv = jnp.float32(1.0) / total
        delta = mixed * inv
        p = e * jnp.where(live, inv, jnp.float32(0.0))
        p_b = p.astype(jnp.bfloat16)
        ds = (p * (dp - delta)).astype(jnp.bfloat16)
        att = dot(vals_t[head], p_b, ((1,), (0,)))
        dq = dot(keys_t[head], ds, ((1,), (0,))) * jnp.float32(SCALE)
        return p_b, ds, att, dq

    def step(i, carry):
        head = i // (GROUP // STEP)
        qs, gs, ps, dss = [], [], [], []
        for j in range(STEP):
            col = pl.multiple_of((i * STEP + j) * HEAD_DIM, HEAD_DIM)
            gcol = pl.multiple_of(WIDE + (i * STEP + j) * HEAD_DIM, HEAD_DIM)
            q = jnp.concatenate([r[:, pl.ds(col, HEAD_DIM)] for r in ins], 0)
            g = jnp.concatenate([r[:, pl.ds(gcol, HEAD_DIM)] for r in ins], 0)
            p_b, ds, att, dq = one(head, q, g)
            att = att.T.astype(jnp.bfloat16)
            dq = dq.T.astype(jnp.bfloat16)
            for x in range(QUART):
                outs[x][:, pl.ds(col, HEAD_DIM)] = att[x * ROWS : (x + 1) * ROWS]
                outs[x][:, pl.ds(gcol, HEAD_DIM)] = dq[x * ROWS : (x + 1) * ROWS]
            qs.append(q)
            gs.append(g)
            ps.append(p_b)
            dss.append(ds)
        k_acc[head] += dot(jnp.concatenate(dss, 1), jnp.concatenate(qs, 0), ((1,), (0,)))
        v_acc[head] += dot(jnp.concatenate(ps, 1), jnp.concatenate(gs, 0), ((1,), (0,)))
        return carry

    lax.fori_loop(0, PAIR * GROUP // STEP, step, 0)

    for head in range(PAIR):
        col = 2 * WIDE + head * HEAD_DIM
        k_grad = (k_acc[head] * jnp.float32(SCALE)).astype(jnp.bfloat16)
        v_grad = v_acc[head].astype(jnp.bfloat16)
        danc_ref[head] = k_grad[0 : ANC * BLK]
        danc_ref[PAIR + head] = v_grad[0 : ANC * BLK]
        for x in range(QUART):
            at = ANC * BLK + x * ROWS
            outs[x][:, col : col + HEAD_DIM] = k_grad[at : at + ROWS]
            outs[x][:, col + NARROW : col + NARROW + HEAD_DIM] = v_grad[at : at + ROWS]


def attention(info, packs, anc):
    cells = PAIR * GROUP * KEYS * BLK
    return pl.pallas_call(
        attention_kernel,
        out_shape=tuple(jax.ShapeDtypeStruct((ROWS, PACK), jnp.bfloat16) for _ in range(QUART))
        + (jax.ShapeDtypeStruct((2 * PAIR, ANC * BLK, HEAD_DIM), jnp.bfloat16),),
        in_specs=[smem()] + whole(QUART + 1),
        out_specs=tuple(whole(QUART + 1)),
        scratch_shapes=[
            pltpu.VMEM((PAIR, KEYS, HEAD_DIM), jnp.bfloat16),
            pltpu.VMEM((PAIR, KEYS, HEAD_DIM), jnp.bfloat16),
            pltpu.VMEM((PAIR, HEAD_DIM, KEYS), jnp.bfloat16),
            pltpu.VMEM((PAIR, HEAD_DIM, KEYS), jnp.bfloat16),
            pltpu.VMEM((KEYS, BLK), jnp.float32),
            pltpu.VMEM((PAIR, KEYS, HEAD_DIM), jnp.float32),
            pltpu.VMEM((PAIR, KEYS, HEAD_DIM), jnp.float32),
        ],
        compiler_params=pltpu.CompilerParams(vmem_limit_bytes=VMEM),
        cost_estimate=pl.CostEstimate(
            flops=10 * cells * HEAD_DIM, bytes_accessed=6 * 1024 * 1024, transcendentals=cells
        ),
    )(info, *packs, anc)


def place_kernel(info_ref, in0, in1, in2, in3, att_ref, dq_ref, dkv_ref):
    me = info_ref[0]
    for x, ref in enumerate((in0, in1, in2, in3)):
        j = me ^ x
        wide = pl.ds(pl.multiple_of(j * WIDE, WIDE), WIDE)
        att_ref[:, wide] = ref[:, 0:WIDE]
        dq_ref[:, wide] = ref[:, WIDE : 2 * WIDE]
        for kv in range(2):
            narrow = pl.ds(pl.multiple_of((kv * QUART + j) * NARROW, NARROW), NARROW)
            dkv_ref[:, narrow] = ref[:, 2 * WIDE + kv * NARROW : 2 * WIDE + (kv + 1) * NARROW]


def place_pieces(info, packs):
    return pl.pallas_call(
        place_kernel,
        out_shape=(
            jax.ShapeDtypeStruct((ROWS, QUART * WIDE), jnp.bfloat16),
            jax.ShapeDtypeStruct((ROWS, QUART * WIDE), jnp.bfloat16),
            jax.ShapeDtypeStruct((ROWS, 2 * QUART * NARROW), jnp.bfloat16),
        ),
        in_specs=[smem()] + whole(QUART),
        out_specs=tuple(whole(3)),
        compiler_params=pltpu.CompilerParams(vmem_limit_bytes=VMEM),
    )(info, *packs)


def partners(x):
    return [(i, i ^ x) for i in range(QUART)]


def body(queries, keys, values, out_grad, ancestors, depths, lengths):
    zh, half, me = lax.axis_index("zh"), lax.axis_index("b"), lax.axis_index("h")
    ctx = (zh * 4 + lax.axis_index("x")) * 4 + lax.axis_index("y")

    tiles = jnp.stack([keys, values]).reshape(2, 8, 8, QUART, PAIR, HEAD_DIM)
    tiles = jnp.transpose(tiles, (0, 4, 1, 3, 2, 5)).reshape(RELAYS * QUART, 8, HEAD_DIM)
    own = lax.all_to_all(tiles, ("x", "y", "b", "h"), 0, 0, tiled=True)
    own = own.reshape(OWN, PIECE, HEAD_DIM)
    prev = lax.ppermute(own[OWN - PREV :], "zh", [(i, i + 1) for i in range(3)])
    lists = lax.all_gather(ancestors, ("x", "y"), axis=0, tiled=True)
    idx = jnp.clip(lists - zh * OWN + PREV, 0, PREV + OWN - 1).reshape(-1)
    sent = gather_pieces(idx, prev, own).reshape(RELAYS, ANC * PIECE, HEAD_DIM)
    anc = lax.all_to_all(sent, ("x", "y", "b"), 0, 0, tiled=True)
    anc = anc.reshape(2 * PAIR, ANC * BLK, HEAD_DIM)

    def pack(x):
        j = me ^ x
        parts = [
            lax.dynamic_slice(queries, (0, j * WIDE), (ROWS, WIDE)),
            lax.dynamic_slice(out_grad, (0, j * WIDE), (ROWS, WIDE)),
            lax.dynamic_slice(keys, (0, j * NARROW), (ROWS, NARROW)),
            lax.dynamic_slice(values, (0, j * NARROW), (ROWS, NARROW)),
        ]
        return jnp.concatenate(parts, 1)

    packs = [pack(x) for x in range(QUART)]
    packs = [packs[0]] + [lax.ppermute(packs[x], "h", partners(x)) for x in range(1, QUART)]

    mine = lax.dynamic_index_in_dim(ancestors, half, 0, keepdims=False)
    depth = lax.dynamic_index_in_dim(depths, half, 0, keepdims=False)
    anc_len = jnp.where(jnp.arange(ANC, dtype=jnp.int32) < depth, lengths[mine], 0)
    own_len = lax.dynamic_index_in_dim(lengths, ctx * BLOCKS + half, 0, keepdims=True)
    info = jnp.concatenate([me.astype(jnp.int32)[None], own_len, anc_len])
    *grads, danc = attention(info, packs, anc)

    danc = danc.reshape(RELAYS, ANC * PIECE, HEAD_DIM)
    terms = lax.all_to_all(danc, ("x", "y", "b"), 0, 0, tiled=True)
    back, total = scatter_pieces(idx, terms.reshape(RELAYS * ANC, PIECE, HEAD_DIM))
    back = lax.ppermute(back, "zh", [(i + 1, i) for i in range(3)])
    total = total.at[OWN - PREV :].add(back.astype(jnp.float32)).astype(jnp.bfloat16)
    total = total.reshape(RELAYS * QUART, 8, HEAD_DIM)
    tiles = lax.all_to_all(total, ("x", "y", "b", "h"), 0, 0, tiled=True)
    tiles = tiles.reshape(2, PAIR, 8, QUART, 8, HEAD_DIM)
    tiles = jnp.transpose(tiles, (0, 2, 4, 3, 1, 5)).reshape(2, ROWS, QUART * NARROW)

    grads = [grads[0]] + [lax.ppermute(grads[x], "h", partners(x)) for x in range(1, QUART)]
    attended, q_grad, own_grad = place_pieces(info, grads)
    own_grad = own_grad.reshape(ROWS, 2, QUART * NARROW).astype(jnp.float32)
    k_grad = (tiles[0].astype(jnp.float32) + own_grad[:, 0]).astype(jnp.bfloat16)
    v_grad = (tiles[1].astype(jnp.float32) + own_grad[:, 1]).astype(jnp.bfloat16)
    return (attended, q_grad, k_grad, v_grad)


def solution(mesh):
    mesh = Mesh(mesh.devices.reshape(4, 4, 4, BLOCKS, QUART), ("zh", "x", "y", "b", "h"))
    ctx = ("zh", "x", "y")
    rows = P(ctx + ("b", "h"), None)
    in_specs = (rows, rows, rows, rows, P(ctx, None), P(ctx), P())
    return jax.shard_map(
        body, mesh=mesh, in_specs=in_specs, out_specs=(rows,) * 4, check_vma=False
    )
```

```python
import functools

import jax
import jax.numpy as jnp
from jax import lax
from jax.experimental import pallas as pl
from jax.experimental.pallas import tpu as pltpu
from jax.sharding import Mesh
from jax.sharding import PartitionSpec as P

HEAD_DIM = 128
BLK = 256
ANC = 2
W = 4
QUART = 4
GROUP = 8
PAIR = 2
ROWS = BLK // QUART
WIDE = GROUP * HEAD_DIM
MAIN = WIDE + 2 * HEAD_DIM
PACK = MAIN + WIDE
NOTE = 16
PLANE = 16
BLOCKS = 2
PREV = (W - 1) * BLOCKS
OWN = PLANE * BLOCKS
RELAYS = PLANE * BLOCKS
TP = BLOCKS * QUART
PIECE = BLK // 8
KEYS = ANC * BLK + BLK
STEP = 4
NEG = -1e30
LOG2E = 1.4426950408889634
SCALE = HEAD_DIM ** (-0.5)
VMEM = 48 * 1024 * 1024


def whole(count):
    return [pl.BlockSpec(memory_space=pltpu.VMEM)] * count


def smem():
    return pl.BlockSpec(memory_space=pltpu.SMEM)


def gather_kernel(idx_ref, prev_ref, own_ref, out_ref, table):
    table[0:PREV] = prev_ref[...]
    for block in range(OWN):
        at = block % BLOCKS * PIECE
        table[PREV + block] = own_ref[block // BLOCKS, at : at + PIECE]
    for entry in range(RELAYS * ANC):
        out_ref[entry] = table[idx_ref[entry]]


def gather_pieces(idx, prev, own):
    return pl.pallas_call(
        gather_kernel,
        out_shape=jax.ShapeDtypeStruct((RELAYS * ANC, PIECE, HEAD_DIM), jnp.bfloat16),
        in_specs=[smem()] + whole(2),
        out_specs=whole(1)[0],
        scratch_shapes=[pltpu.VMEM((PREV + OWN, PIECE, HEAD_DIM), jnp.bfloat16)],
        compiler_params=pltpu.CompilerParams(vmem_limit_bytes=VMEM),
    )(idx, prev, own)


def scatter_kernel(idx_ref, terms_ref, prev_ref, own_ref, table):
    table[...] = jnp.zeros_like(table)
    for entry in range(RELAYS * ANC):
        place = idx_ref[entry]
        table[place] = table[place] + terms_ref[entry].astype(jnp.float32)
    prev_ref[...] = table[0:PREV].astype(jnp.bfloat16)
    own_ref[...] = table[PREV:]


def scatter_pieces(idx, terms):
    return pl.pallas_call(
        scatter_kernel,
        out_shape=(
            jax.ShapeDtypeStruct((PREV, PIECE, HEAD_DIM), jnp.bfloat16),
            jax.ShapeDtypeStruct((OWN, PIECE, HEAD_DIM), jnp.float32),
        ),
        in_specs=[smem()] + whole(1),
        out_specs=tuple(whole(2)),
        scratch_shapes=[pltpu.VMEM((PREV + OWN, PIECE, HEAD_DIM), jnp.float32)],
        compiler_params=pltpu.CompilerParams(vmem_limit_bytes=VMEM),
    )(idx, terms)


def dot(a, b, dims):
    return lax.dot_general(a, b, (dims, ((), ())), preferred_element_type=jnp.float32)


def attention_kernel(
    head, info_ref, in0, in1, in2, in3, anc_ref, first_ref, out0, out1, out2, out3, danc_ref,
    key, val, key_t, val_t, bias, k_acc, v_acc,
):
    ins = (in0, in1, in2, in3)
    outs = (out0, out1, out2, out3)
    base = head * PACK
    me = info_ref[0]
    own_len = info_ref[1]

    def own_pos(shape, dim):
        row = lax.broadcasted_iota(jnp.int32, shape, dim)
        return ((row // ROWS) ^ me) * ROWS + row % ROWS

    row = lax.broadcasted_iota(jnp.int32, (ANC * BLK, BLK), 0)
    slot = (row // PIECE) % ANC
    place = ((row // 8) % QUART) * ROWS + (row // (ANC * PIECE)) * 8 + row % 8
    limit = jnp.where(slot == 0, info_ref[2], info_ref[3])
    bias[0 : ANC * BLK] = jnp.where(place < limit, jnp.float32(0.0), jnp.float32(NEG))
    key_pos = own_pos((BLK, BLK), 0)
    query_pos = own_pos((BLK, BLK), 1)
    bias[ANC * BLK :] = jnp.where(
        (key_pos <= query_pos) & (key_pos < own_len), jnp.float32(0.0), jnp.float32(NEG)
    )
    live = own_pos((1, BLK), 1) < own_len

    key[0 : ANC * BLK] = anc_ref[head]
    val[0 : ANC * BLK] = anc_ref[PAIR + head]
    for x in range(QUART):
        at = ANC * BLK + x * ROWS
        key[at : at + ROWS] = ins[x][:, base + WIDE : base + WIDE + HEAD_DIM]
        val[at : at + ROWS] = ins[x][:, base + WIDE + HEAD_DIM : base + MAIN]
    key_t[...] = key[...].T
    val_t[...] = val[...].T

    def one(q, g):
        s = dot(key[...], q, ((1,), (1,))) + bias[...]
        dp = dot(val[...], g, ((1,), (1,)))
        top = jnp.max(s, axis=0, keepdims=True)
        e = jnp.exp2((s - top) * jnp.float32(SCALE * LOG2E))
        total = jnp.sum(e, axis=0, keepdims=True)
        mixed = jnp.sum(e * dp, axis=0, keepdims=True)
        inv = jnp.float32(1.0) / total
        delta = mixed * inv
        p = e * jnp.where(live, inv, jnp.float32(0.0))
        p_b = p.astype(jnp.bfloat16)
        ds = (p * (dp - delta)).astype(jnp.bfloat16)
        att = dot(val_t[...], p_b, ((1,), (0,)))
        dq = dot(key_t[...], ds, ((1,), (0,))) * jnp.float32(SCALE)
        return p_b, ds, att, dq

    for i in range(GROUP // STEP):
        qs, gs, ps, dss = [], [], [], []
        for j in range(STEP):
            col = (i * STEP + j) * HEAD_DIM
            at = base + col
            q = jnp.concatenate([r[:, at : at + HEAD_DIM] for r in ins], 0)
            at = base + MAIN + col
            g = jnp.concatenate([r[:, at : at + HEAD_DIM] for r in ins], 0)
            p_b, ds, att, dq = one(q, g)
            att = att.T.astype(jnp.bfloat16)
            dq = dq.T.astype(jnp.bfloat16)
            for x in range(QUART):
                outs[x][:, col : col + HEAD_DIM] = att[x * ROWS : (x + 1) * ROWS]
                outs[x][:, MAIN + col : MAIN + col + HEAD_DIM] = dq[x * ROWS : (x + 1) * ROWS]
            qs.append(q)
            gs.append(g)
            ps.append(p_b)
            dss.append(ds)
        dk = dot(jnp.concatenate(dss, 1), jnp.concatenate(qs, 0), ((1,), (0,)))
        dv = dot(jnp.concatenate(ps, 1), jnp.concatenate(gs, 0), ((1,), (0,)))
        k_acc[...] = dk if i == 0 else k_acc[...] + dk
        v_acc[...] = dv if i == 0 else v_acc[...] + dv

    k_grad = (k_acc[...] * jnp.float32(SCALE)).astype(jnp.bfloat16)
    v_grad = v_acc[...].astype(jnp.bfloat16)
    if head == 0:
        danc_ref[0] = k_grad[0 : ANC * BLK]
        danc_ref[1] = v_grad[0 : ANC * BLK]
    else:
        danc_ref[0] = first_ref[0]
        danc_ref[1] = k_grad[0 : ANC * BLK]
        danc_ref[2] = first_ref[1]
        danc_ref[3] = v_grad[0 : ANC * BLK]
    for x in range(QUART):
        at = ANC * BLK + x * ROWS
        outs[x][:, WIDE : WIDE + HEAD_DIM] = k_grad[at : at + ROWS]
        outs[x][:, WIDE + HEAD_DIM : MAIN] = v_grad[at : at + ROWS]


def attention(head, info, packs, anc, first):
    return pl.pallas_call(
        functools.partial(attention_kernel, head),
        out_shape=tuple(jax.ShapeDtypeStruct((ROWS, PACK), jnp.bfloat16) for _ in range(QUART))
        + (jax.ShapeDtypeStruct((2 * (head + 1), ANC * BLK, HEAD_DIM), jnp.bfloat16),),
        in_specs=[smem()] + whole(QUART + 2),
        out_specs=tuple(whole(QUART + 1)),
        scratch_shapes=[
            pltpu.VMEM((KEYS, HEAD_DIM), jnp.bfloat16),
            pltpu.VMEM((KEYS, HEAD_DIM), jnp.bfloat16),
            pltpu.VMEM((HEAD_DIM, KEYS), jnp.bfloat16),
            pltpu.VMEM((HEAD_DIM, KEYS), jnp.bfloat16),
            pltpu.VMEM((KEYS, BLK), jnp.float32),
            pltpu.VMEM((KEYS, HEAD_DIM), jnp.float32),
            pltpu.VMEM((KEYS, HEAD_DIM), jnp.float32),
        ],
        compiler_params=pltpu.CompilerParams(vmem_limit_bytes=VMEM),
    )(info, *packs, anc, first)


def pack_kernel(info_ref, q_ref, k_ref, v_ref, g_ref, *outs):
    for x in range(QUART):
        for head in range(PAIR):
            j = (info_ref[0] ^ x) * PAIR + head
            out, base = outs[x], head * PACK
            wide = pl.ds(pl.multiple_of(j * WIDE, WIDE), WIDE)
            narrow = pl.ds(pl.multiple_of(j * HEAD_DIM, HEAD_DIM), HEAD_DIM)
            out[:, base : base + WIDE] = q_ref[:, wide]
            out[:, base + WIDE : base + WIDE + HEAD_DIM] = k_ref[:, narrow]
            out[:, base + WIDE + HEAD_DIM : base + MAIN] = v_ref[:, narrow]
            out[:, base + MAIN : base + PACK] = g_ref[:, wide]


def pack_pieces(info, queries, keys, values, out_grad):
    return pl.pallas_call(
        pack_kernel,
        out_shape=tuple(
            jax.ShapeDtypeStruct((ROWS, PAIR * PACK), jnp.bfloat16) for _ in range(QUART)
        ),
        in_specs=[smem()] + whole(4),
        out_specs=tuple(whole(QUART)),
        compiler_params=pltpu.CompilerParams(vmem_limit_bytes=VMEM),
    )(info, queries, keys, values, out_grad)


def place_kernel(info_ref, *refs):
    ins, (att_ref, dq_ref, dkv_ref) = refs[: QUART * PAIR], refs[QUART * PAIR :]
    for x in range(QUART):
        for head in range(PAIR):
            j = (info_ref[0] ^ x) * PAIR + head
            ref = ins[x * PAIR + head]
            wide = pl.ds(pl.multiple_of(j * WIDE, WIDE), WIDE)
            att_ref[:, wide] = ref[:, 0:WIDE]
            dq_ref[:, wide] = ref[:, MAIN:PACK]
            for kv in range(2):
                at = kv * QUART * PAIR * HEAD_DIM + j * HEAD_DIM
                narrow = pl.ds(pl.multiple_of(at, HEAD_DIM), HEAD_DIM)
                col = WIDE + kv * HEAD_DIM
                dkv_ref[:, narrow] = ref[:, col : col + HEAD_DIM]


def place_pieces(info, packs):
    heads = QUART * PAIR
    return pl.pallas_call(
        place_kernel,
        out_shape=(
            jax.ShapeDtypeStruct((ROWS, heads * WIDE), jnp.bfloat16),
            jax.ShapeDtypeStruct((ROWS, heads * WIDE), jnp.bfloat16),
            jax.ShapeDtypeStruct((ROWS, 2 * heads * HEAD_DIM), jnp.bfloat16),
        ),
        in_specs=[smem()] + whole(heads),
        out_specs=tuple(whole(3)),
        compiler_params=pltpu.CompilerParams(vmem_limit_bytes=VMEM),
    )(info, *packs)


def partners(x):
    return [(i, i ^ x) for i in range(QUART)]


def body(queries, keys, values, out_grad, ancestors, depths, lengths):
    zh, half, me = lax.axis_index("zh"), lax.axis_index("b"), lax.axis_index("h")
    ctx = (zh * 4 + lax.axis_index("x")) * 4 + lax.axis_index("y")

    tiles = jnp.stack([keys, values]).reshape(2, 4, BLOCKS, 8, QUART, PAIR, HEAD_DIM)
    tiles = jnp.transpose(tiles, (2, 4, 0, 5, 1, 3, 6)).reshape(TP, PLANE * 8, HEAD_DIM)
    tiles = lax.all_to_all(tiles, ("b", "h"), 0, 0, tiled=True)
    tiles = jnp.transpose(tiles.reshape(TP, PLANE, 8, HEAD_DIM), (1, 0, 2, 3))
    tiles = tiles.reshape(PLANE, TP * 8, HEAD_DIM)
    note = ancestors.reshape(1, 1, BLOCKS * ANC).astype(jnp.bfloat16)
    note = jnp.pad(note, ((0, 0), (0, NOTE - 1), (0, HEAD_DIM - BLOCKS * ANC)))
    tiles = jnp.concatenate([tiles, jnp.broadcast_to(note, (PLANE, NOTE, HEAD_DIM))], 1)
    own = lax.all_to_all(tiles, ("x", "y"), 0, 0, tiled=True)
    def swap(x, part):
        return lax.ppermute(part, "h", partners(x)) if x else part

    mine = lax.dynamic_index_in_dim(ancestors, half, 0, keepdims=False)
    depth = lax.dynamic_index_in_dim(depths, half, 0, keepdims=False)
    anc_len = jnp.where(jnp.arange(ANC, dtype=jnp.int32) < depth, lengths[mine], 0)
    own_len = lax.dynamic_index_in_dim(lengths, ctx * BLOCKS + half, 0, keepdims=True)
    info = jnp.concatenate([me.astype(jnp.int32)[None], own_len, anc_len])
    packs = pack_pieces(me.astype(jnp.int32)[None], queries, keys, values, out_grad)
    packs = [swap(x, packs[x]) for x in range(QUART)]

    last = own[PLANE - W + 1 :, : TP * 8].reshape(PREV, PIECE, HEAD_DIM)
    prev = lax.ppermute(last, "zh", [(i, i + 1) for i in range(3)])
    own, *packs[2:] = lax.optimization_barrier((own, *packs[2:]))
    lists = own[:, TP * 8, : BLOCKS * ANC].astype(jnp.int32).reshape(-1)
    idx = jnp.clip(lists - zh * OWN + PREV, 0, PREV + OWN - 1)
    sent = gather_pieces(idx, prev, own).reshape(RELAYS, ANC * PIECE, HEAD_DIM)
    anc = lax.all_to_all(sent, ("x", "y", "b"), 0, 0, tiled=True)
    anc = anc.reshape(2 * PAIR, ANC * BLK, HEAD_DIM)

    *outs0, danc = attention(0, info, packs, anc, anc)
    *outs1, danc = attention(1, info, packs, anc, danc)
    outs0 = [swap(x, outs0[x]) for x in range(QUART)]
    danc, *outs0[2:] = lax.optimization_barrier((danc, *outs0[2:]))

    danc = danc.reshape(RELAYS, ANC * PIECE, HEAD_DIM)
    terms = lax.all_to_all(danc, ("x", "y", "b"), 0, 0, tiled=True)
    outs1 = [swap(x, outs1[x]) for x in range(QUART)]
    back, total = scatter_pieces(idx, terms.reshape(RELAYS * ANC, PIECE, HEAD_DIM))
    back = lax.ppermute(back, "zh", [(i + 1, i) for i in range(3)])
    back, *outs1[2:] = lax.optimization_barrier((back, *outs1[2:]))
    total = total.at[OWN - PREV :].add(back.astype(jnp.float32)).astype(jnp.bfloat16)
    total = total.reshape(PLANE, TP * 8, HEAD_DIM)
    tiles = lax.all_to_all(total, ("x", "y"), 0, 0, tiled=True)
    tiles, outs0[1], outs1[1] = lax.optimization_barrier((tiles, outs0[1], outs1[1]))
    tiles = jnp.transpose(tiles.reshape(PLANE, TP, 8, HEAD_DIM), (1, 0, 2, 3))
    tiles = lax.all_to_all(tiles.reshape(TP, PLANE * 8, HEAD_DIM), ("b", "h"), 0, 0, tiled=True)
    tiles = tiles.reshape(BLOCKS, QUART, 2, PAIR, 4, 8, HEAD_DIM)
    tiles = jnp.transpose(tiles, (2, 4, 0, 5, 1, 3, 6)).reshape(2, ROWS, QUART * PAIR * HEAD_DIM)

    outs = [out for pair in zip(outs0, outs1) for out in pair]
    attended, q_grad, own_grad = place_pieces(info, outs)
    own_grad = own_grad.reshape(ROWS, 2, QUART * PAIR * HEAD_DIM).astype(jnp.float32)
    k_grad = (tiles[0].astype(jnp.float32) + own_grad[:, 0]).astype(jnp.bfloat16)
    v_grad = (tiles[1].astype(jnp.float32) + own_grad[:, 1]).astype(jnp.bfloat16)
    return (attended, q_grad, k_grad, v_grad)


def solution(mesh):
    mesh = Mesh(mesh.devices.reshape(4, 4, 4, BLOCKS, QUART), ("zh", "x", "y", "b", "h"))
    ctx = ("zh", "x", "y")
    rows = P(ctx + ("b", "h"), None)
    in_specs = (rows, rows, rows, rows, P(ctx, None), P(ctx), P())
    return jax.shard_map(
        body, mesh=mesh, in_specs=in_specs, out_specs=(rows,) * 4, check_vma=False
    )
```

```python
import functools

import jax
import jax.numpy as jnp
from jax import lax
from jax.experimental import pallas as pl
from jax.experimental.pallas import tpu as pltpu
from jax.sharding import Mesh
from jax.sharding import PartitionSpec as P

HEAD_DIM = 128
BLK = 256
ANC = 2
W = 4
QUART = 4
GROUP = 8
PAIR = 2
ROWS = BLK // QUART
WIDE = GROUP * HEAD_DIM
MAIN = WIDE + 2 * HEAD_DIM
PACK = MAIN + WIDE
COLS = (PACK, PACK, 2 * PACK)
NOTE = 16
PLANE = 16
BLOCKS = 2
PREV = (W - 1) * BLOCKS
OWN = PLANE * BLOCKS
RELAYS = PLANE * BLOCKS
TP = BLOCKS * QUART
PIECE = BLK // 8
KEYS = ANC * BLK + BLK
STEP = 4
NEG = -1e30
LOG2E = 1.4426950408889634
SCALE = HEAD_DIM ** (-0.5)
MIB = 1024 * 1024


def whole(count):
    return [pl.BlockSpec(memory_space=pltpu.VMEM)] * count


def smem():
    return pl.BlockSpec(memory_space=pltpu.SMEM)


def gather_kernel(idx_ref, prev_ref, own_ref, out_ref, table):
    table[0:PREV] = prev_ref[...]
    for block in range(OWN):
        at = block % BLOCKS * PIECE
        table[PREV + block] = own_ref[block // BLOCKS, at : at + PIECE]
    for entry in range(RELAYS * ANC):
        out_ref[entry] = table[idx_ref[entry]]


def gather_pieces(idx, prev, own):
    return pl.pallas_call(
        gather_kernel,
        out_shape=jax.ShapeDtypeStruct((RELAYS * ANC, PIECE, HEAD_DIM), jnp.bfloat16),
        in_specs=[smem()] + whole(2),
        out_specs=whole(1)[0],
        scratch_shapes=[pltpu.VMEM((PREV + OWN, PIECE, HEAD_DIM), jnp.bfloat16)],
        compiler_params=pltpu.CompilerParams(vmem_limit_bytes=8 * MIB),
    )(idx, prev, own)


def scatter_kernel(idx_ref, terms_ref, prev_ref, last_ref, own_ref, table):
    table[...] = jnp.zeros_like(table)
    for entry in range(RELAYS * ANC):
        place = idx_ref[entry]
        table[place] = table[place] + terms_ref[entry].astype(jnp.float32)
    prev_ref[...] = table[0:PREV].astype(jnp.bfloat16)
    last_ref[...] = table[OWN:]
    own_ref[...] = table[PREV:].astype(jnp.bfloat16)


def scatter_pieces(idx, terms):
    return pl.pallas_call(
        scatter_kernel,
        out_shape=(
            jax.ShapeDtypeStruct((PREV, PIECE, HEAD_DIM), jnp.bfloat16),
            jax.ShapeDtypeStruct((PREV, PIECE, HEAD_DIM), jnp.float32),
            jax.ShapeDtypeStruct((OWN, PIECE, HEAD_DIM), jnp.bfloat16),
        ),
        in_specs=[smem()] + whole(1),
        out_specs=tuple(whole(3)),
        scratch_shapes=[pltpu.VMEM((PREV + OWN, PIECE, HEAD_DIM), jnp.float32)],
        compiler_params=pltpu.CompilerParams(vmem_limit_bytes=8 * MIB),
    )(idx, terms)


def dot(a, b, dims):
    return lax.dot_general(a, b, (dims, ((), ())), preferred_element_type=jnp.float32)


def attention_kernel(
    head, info_ref, in0, in1, in2, in3, anc_ref, first_ref, out0, out1, far_ref, danc_ref,
    key, val, key_t, val_t, bias, k_acc, v_acc,
):
    ins = (in0, in1, in2, in3)
    outs = ((out0, 0), (out1, 0), (far_ref, 0), (far_ref, PACK))
    base = head * PACK
    me = info_ref[0]
    own_len = info_ref[1]

    def own_pos(shape, dim):
        row = lax.broadcasted_iota(jnp.int32, shape, dim)
        return ((row // ROWS) ^ me) * ROWS + row % ROWS

    row = lax.broadcasted_iota(jnp.int32, (ANC * BLK, BLK), 0)
    slot = (row // PIECE) % ANC
    place = ((row // 8) % QUART) * ROWS + (row // (ANC * PIECE)) * 8 + row % 8
    limit = jnp.where(slot == 0, info_ref[2], info_ref[3])
    bias[0 : ANC * BLK] = jnp.where(place < limit, jnp.float32(0.0), jnp.float32(NEG))
    key_pos = own_pos((BLK, BLK), 0)
    query_pos = own_pos((BLK, BLK), 1)
    bias[ANC * BLK :] = jnp.where(
        (key_pos <= query_pos) & (key_pos < own_len), jnp.float32(0.0), jnp.float32(NEG)
    )
    live = own_pos((1, BLK), 1) < own_len

    key[0 : ANC * BLK] = anc_ref[head]
    val[0 : ANC * BLK] = anc_ref[PAIR + head]
    for x in range(QUART):
        at = ANC * BLK + x * ROWS
        key[at : at + ROWS] = ins[x][:, base + WIDE : base + WIDE + HEAD_DIM]
        val[at : at + ROWS] = ins[x][:, base + WIDE + HEAD_DIM : base + MAIN]
    key_t[...] = key[...].T
    val_t[...] = val[...].T

    def one(q, g):
        s = dot(key[...], q, ((1,), (1,))) + bias[...]
        dp = dot(val[...], g, ((1,), (1,)))
        top = jnp.max(s, axis=0, keepdims=True)
        e = jnp.exp2((s - top) * jnp.float32(SCALE * LOG2E))
        total = jnp.sum(e, axis=0, keepdims=True)
        mixed = jnp.sum(e * dp, axis=0, keepdims=True)
        inv = jnp.float32(1.0) / total
        delta = mixed * inv
        p = e * jnp.where(live, inv, jnp.float32(0.0))
        p_b = p.astype(jnp.bfloat16)
        ds = (p * (dp - delta)).astype(jnp.bfloat16)
        att = dot(val_t[...], p_b, ((1,), (0,)))
        dq = dot(key_t[...], ds, ((1,), (0,))) * jnp.float32(SCALE)
        return p_b, ds, att, dq

    for i in range(GROUP // STEP):
        qs, gs, ps, dss = [], [], [], []
        for j in range(STEP):
            col = (i * STEP + j) * HEAD_DIM
            at = base + col
            q = jnp.concatenate([r[:, at : at + HEAD_DIM] for r in ins], 0)
            at = base + MAIN + col
            g = jnp.concatenate([r[:, at : at + HEAD_DIM] for r in ins], 0)
            p_b, ds, att, dq = one(q, g)
            att = att.T.astype(jnp.bfloat16)
            dq = dq.T.astype(jnp.bfloat16)
            for x in range(QUART):
                out, at = outs[x]
                out[:, at + col : at + col + HEAD_DIM] = att[x * ROWS : (x + 1) * ROWS]
                at = at + MAIN + col
                out[:, at : at + HEAD_DIM] = dq[x * ROWS : (x + 1) * ROWS]
            qs.append(q)
            gs.append(g)
            ps.append(p_b)
            dss.append(ds)
        dk = dot(jnp.concatenate(dss, 1), jnp.concatenate(qs, 0), ((1,), (0,)))
        dv = dot(jnp.concatenate(ps, 1), jnp.concatenate(gs, 0), ((1,), (0,)))
        k_acc[...] = dk if i == 0 else k_acc[...] + dk
        v_acc[...] = dv if i == 0 else v_acc[...] + dv

    k_grad = (k_acc[...] * jnp.float32(SCALE)).astype(jnp.bfloat16)
    v_grad = v_acc[...].astype(jnp.bfloat16)
    if head == 0:
        danc_ref[0] = k_grad[0 : ANC * BLK]
        danc_ref[1] = v_grad[0 : ANC * BLK]
    else:
        danc_ref[0] = first_ref[0]
        danc_ref[1] = k_grad[0 : ANC * BLK]
        danc_ref[2] = first_ref[1]
        danc_ref[3] = v_grad[0 : ANC * BLK]
    for x in range(QUART):
        out, at = outs[x]
        row = ANC * BLK + x * ROWS
        out[:, at + WIDE : at + WIDE + HEAD_DIM] = k_grad[row : row + ROWS]
        out[:, at + WIDE + HEAD_DIM : at + MAIN] = v_grad[row : row + ROWS]


def attention(head, info, packs, anc, first):
    return pl.pallas_call(
        functools.partial(attention_kernel, head),
        out_shape=tuple(jax.ShapeDtypeStruct((ROWS, c), jnp.bfloat16) for c in COLS)
        + (jax.ShapeDtypeStruct((2 * (head + 1), ANC * BLK, HEAD_DIM), jnp.bfloat16),),
        in_specs=[smem()] + whole(QUART + 2),
        out_specs=tuple(whole(len(COLS) + 1)),
        scratch_shapes=[
            pltpu.VMEM((KEYS, HEAD_DIM), jnp.bfloat16),
            pltpu.VMEM((KEYS, HEAD_DIM), jnp.bfloat16),
            pltpu.VMEM((HEAD_DIM, KEYS), jnp.bfloat16),
            pltpu.VMEM((HEAD_DIM, KEYS), jnp.bfloat16),
            pltpu.VMEM((KEYS, BLK), jnp.float32),
            pltpu.VMEM((KEYS, HEAD_DIM), jnp.float32),
            pltpu.VMEM((KEYS, HEAD_DIM), jnp.float32),
        ],
        compiler_params=pltpu.CompilerParams(vmem_limit_bytes=32 * MIB),
    )(info, *packs, anc, first)


def pack_kernel(info_ref, q_ref, k_ref, v_ref, g_ref, *outs):
    for x in range(QUART):
        for head in range(PAIR):
            j = (info_ref[0] ^ x) * PAIR + head
            out, base = outs[x], head * PACK
            wide = pl.ds(pl.multiple_of(j * WIDE, WIDE), WIDE)
            narrow = pl.ds(pl.multiple_of(j * HEAD_DIM, HEAD_DIM), HEAD_DIM)
            out[:, base : base + WIDE] = q_ref[:, wide]
            out[:, base + WIDE : base + WIDE + HEAD_DIM] = k_ref[:, narrow]
            out[:, base + WIDE + HEAD_DIM : base + MAIN] = v_ref[:, narrow]
            out[:, base + MAIN : base + PACK] = g_ref[:, wide]


def pack_pieces(info, queries, keys, values, out_grad):
    return pl.pallas_call(
        pack_kernel,
        out_shape=tuple(
            jax.ShapeDtypeStruct((ROWS, PAIR * PACK), jnp.bfloat16) for _ in range(QUART)
        ),
        in_specs=[smem()] + whole(4),
        out_specs=tuple(whole(QUART)),
        compiler_params=pltpu.CompilerParams(vmem_limit_bytes=12 * MIB),
    )(info, queries, keys, values, out_grad)


def place_kernel(info_ref, *refs):
    ins, (att_ref, dq_ref, dkv_ref) = refs[: QUART * PAIR], refs[QUART * PAIR :]
    for x in range(QUART):
        for head in range(PAIR):
            j = (info_ref[0] ^ x) * PAIR + head
            ref = ins[x * PAIR + head]
            wide = pl.ds(pl.multiple_of(j * WIDE, WIDE), WIDE)
            att_ref[:, wide] = ref[:, 0:WIDE]
            dq_ref[:, wide] = ref[:, MAIN:PACK]
            for kv in range(2):
                at = kv * QUART * PAIR * HEAD_DIM + j * HEAD_DIM
                narrow = pl.ds(pl.multiple_of(at, HEAD_DIM), HEAD_DIM)
                col = WIDE + kv * HEAD_DIM
                dkv_ref[:, narrow] = ref[:, col : col + HEAD_DIM]


def place_pieces(info, packs):
    heads = QUART * PAIR
    return pl.pallas_call(
        place_kernel,
        out_shape=(
            jax.ShapeDtypeStruct((ROWS, heads * WIDE), jnp.bfloat16),
            jax.ShapeDtypeStruct((ROWS, heads * WIDE), jnp.bfloat16),
            jax.ShapeDtypeStruct((ROWS, 2 * heads * HEAD_DIM), jnp.bfloat16),
        ),
        in_specs=[smem()] + whole(heads),
        out_specs=tuple(whole(3)),
        compiler_params=pltpu.CompilerParams(vmem_limit_bytes=12 * MIB),
    )(info, *packs)


def partners(x):
    return [(i, i ^ x) for i in range(QUART)]


def body(queries, keys, values, out_grad, ancestors, depths, lengths):
    zh, half, me = lax.axis_index("zh"), lax.axis_index("b"), lax.axis_index("h")
    ctx = (zh * 4 + lax.axis_index("x")) * 4 + lax.axis_index("y")

    tiles = jnp.stack([keys, values]).reshape(2, 4, BLOCKS, 8, QUART, PAIR, HEAD_DIM)
    tiles = jnp.transpose(tiles, (2, 4, 0, 5, 1, 3, 6)).reshape(TP, PLANE * 8, HEAD_DIM)
    tiles = lax.all_to_all(tiles, ("b", "h"), 0, 0, tiled=True)
    tiles = jnp.transpose(tiles.reshape(TP, PLANE, 8, HEAD_DIM), (1, 0, 2, 3))
    tiles = tiles.reshape(PLANE, TP * 8, HEAD_DIM)
    note = ancestors.reshape(1, 1, BLOCKS * ANC).astype(jnp.bfloat16)
    note = jnp.pad(note, ((0, 0), (0, NOTE - 1), (0, HEAD_DIM - BLOCKS * ANC)))
    tiles = jnp.concatenate([tiles, jnp.broadcast_to(note, (PLANE, NOTE, HEAD_DIM))], 1)
    own = lax.all_to_all(tiles, ("x", "y"), 0, 0, tiled=True)
    def swap(x, part):
        return lax.ppermute(part, "h", partners(x)) if x else part

    mine = lax.dynamic_index_in_dim(ancestors, half, 0, keepdims=False)
    depth = lax.dynamic_index_in_dim(depths, half, 0, keepdims=False)
    anc_len = jnp.where(jnp.arange(ANC, dtype=jnp.int32) < depth, lengths[mine], 0)
    own_len = lax.dynamic_index_in_dim(lengths, ctx * BLOCKS + half, 0, keepdims=True)
    info = jnp.concatenate([me.astype(jnp.int32)[None], own_len, anc_len])
    packs = pack_pieces(me.astype(jnp.int32)[None], queries, keys, values, out_grad)
    packs = [swap(x, packs[x]) for x in range(QUART)]

    last = own[PLANE - W + 1 :, : TP * 8].reshape(PREV, PIECE, HEAD_DIM)
    prev = lax.ppermute(last, "zh", [(i, i + 1) for i in range(3)])
    own, *packs[2:] = lax.optimization_barrier((own, *packs[2:]))
    lists = own[:, TP * 8, : BLOCKS * ANC].astype(jnp.int32).reshape(-1)
    idx = jnp.clip(lists - zh * OWN + PREV, 0, PREV + OWN - 1)
    sent = gather_pieces(idx, prev, own).reshape(RELAYS, ANC * PIECE, HEAD_DIM)
    anc = lax.all_to_all(sent, ("x", "y", "b"), 0, 0, tiled=True)
    anc = anc.reshape(2 * PAIR, ANC * BLK, HEAD_DIM)

    own0, near0, far0, danc = attention(0, info, packs, anc, anc)
    own1, near1, far1, danc = attention(1, info, packs, anc, danc)
    far0 = swap(2, far0)
    danc, far0 = lax.optimization_barrier((danc, far0))
    near0, on0 = swap(1, near0), swap(1, far0[:, PACK:])

    danc = danc.reshape(RELAYS, ANC * PIECE, HEAD_DIM)
    terms = lax.all_to_all(danc, ("x", "y", "b"), 0, 0, tiled=True)
    near1, far1 = swap(1, near1), swap(2, far1)
    back, last, total = scatter_pieces(idx, terms.reshape(RELAYS * ANC, PIECE, HEAD_DIM))
    back = lax.ppermute(back, "zh", [(i + 1, i) for i in range(3)])
    back, near0, on0, far1 = lax.optimization_barrier((back, near0, on0, far1))
    on1 = swap(1, far1[:, PACK:])
    last = (last + back.astype(jnp.float32)).astype(jnp.bfloat16)
    total = total.at[OWN - PREV :].set(last).reshape(RELAYS * QUART, 8, HEAD_DIM)
    tiles = lax.all_to_all(total, ("x", "y", "b", "h"), 0, 0, tiled=True)
    tiles = tiles.reshape(2, PAIR, 4, BLOCKS, QUART, 8, HEAD_DIM)
    tiles = jnp.transpose(tiles, (0, 2, 3, 5, 4, 1, 6)).reshape(2, ROWS, QUART * PAIR * HEAD_DIM)

    outs = (own0, own1, near0, near1, far0, far1, on0, on1)
    attended, q_grad, own_grad = place_pieces(info, outs)
    own_grad = own_grad.reshape(ROWS, 2, QUART * PAIR * HEAD_DIM).astype(jnp.float32)
    k_grad = (tiles[0].astype(jnp.float32) + own_grad[:, 0]).astype(jnp.bfloat16)
    v_grad = (tiles[1].astype(jnp.float32) + own_grad[:, 1]).astype(jnp.bfloat16)
    return (attended, q_grad, k_grad, v_grad)


def solution(mesh):
    mesh = Mesh(mesh.devices.reshape(4, 4, 4, BLOCKS, QUART), ("zh", "x", "y", "b", "h"))
    ctx = ("zh", "x", "y")
    rows = P(ctx + ("b", "h"), None)
    in_specs = (rows, rows, rows, rows, P(ctx, None), P(ctx), P())
    return jax.shard_map(
        body, mesh=mesh, in_specs=in_specs, out_specs=(rows,) * 4, check_vma=False
    )
```

```python
import functools

import jax
import jax.numpy as jnp
from jax import lax
from jax.experimental import pallas as pl
from jax.experimental.pallas import tpu as pltpu
from jax.sharding import Mesh
from jax.sharding import PartitionSpec as P

HEAD_DIM = 128
BLK = 256
ANC = 2
W = 4
QUART = 4
GROUP = 8
PAIR = 2
ROWS = BLK // QUART
WIDE = GROUP * HEAD_DIM
MAIN = WIDE + 2 * HEAD_DIM
PACK = MAIN + WIDE
COLS = (PACK, PACK, 2 * PACK)
NOTE = 16
PLANE = 16
BLOCKS = 2
PREV = (W - 1) * BLOCKS
OWN = PLANE * BLOCKS
RELAYS = PLANE * BLOCKS
TP = BLOCKS * QUART
PIECE = BLK // 8
KEYS = ANC * BLK + BLK
CHUNK = 256
STEP = 4
NEG = -1e30
LOG2E = 1.4426950408889634
SCALE = HEAD_DIM ** (-0.5)
MIB = 1024 * 1024


def whole(count):
    return [pl.BlockSpec(memory_space=pltpu.VMEM)] * count


def smem():
    return pl.BlockSpec(memory_space=pltpu.SMEM)


def gather_kernel(idx_ref, prev_ref, own_ref, out_ref, table):
    table[0:PREV] = prev_ref[...]
    for block in range(OWN):
        at = block % BLOCKS * PIECE
        table[PREV + block] = own_ref[block // BLOCKS, at : at + PIECE]
    for entry in range(RELAYS * ANC):
        out_ref[entry] = table[idx_ref[entry]]


def gather_pieces(idx, prev, own):
    return pl.pallas_call(
        gather_kernel,
        out_shape=jax.ShapeDtypeStruct((RELAYS * ANC, PIECE, HEAD_DIM), jnp.bfloat16),
        in_specs=[smem()] + whole(2),
        out_specs=whole(1)[0],
        scratch_shapes=[pltpu.VMEM((PREV + OWN, PIECE, HEAD_DIM), jnp.bfloat16)],
        compiler_params=pltpu.CompilerParams(vmem_limit_bytes=8 * MIB),
    )(idx, prev, own)


def scatter_kernel(idx_ref, terms_ref, prev_ref, last_ref, own_ref, table):
    table[...] = jnp.zeros_like(table)
    for entry in range(RELAYS * ANC):
        place = idx_ref[entry]
        table[place] = table[place] + terms_ref[entry].astype(jnp.float32)
    prev_ref[...] = table[0:PREV].astype(jnp.bfloat16)
    last_ref[...] = table[OWN:]
    own_ref[...] = table[PREV:].astype(jnp.bfloat16)


def scatter_pieces(idx, terms):
    return pl.pallas_call(
        scatter_kernel,
        out_shape=(
            jax.ShapeDtypeStruct((PREV, PIECE, HEAD_DIM), jnp.bfloat16),
            jax.ShapeDtypeStruct((PREV, PIECE, HEAD_DIM), jnp.float32),
            jax.ShapeDtypeStruct((OWN, PIECE, HEAD_DIM), jnp.bfloat16),
        ),
        in_specs=[smem()] + whole(1),
        out_specs=tuple(whole(3)),
        scratch_shapes=[pltpu.VMEM((PREV + OWN, PIECE, HEAD_DIM), jnp.float32)],
        compiler_params=pltpu.CompilerParams(vmem_limit_bytes=8 * MIB),
    )(idx, terms)


def dot(a, b, dims):
    return lax.dot_general(a, b, (dims, ((), ())), preferred_element_type=jnp.float32)


def bias_kernel(info_ref, bias):
    me = info_ref[0]
    own_len = info_ref[1]

    def own_pos(shape, dim):
        row = lax.broadcasted_iota(jnp.int32, shape, dim)
        return ((row // ROWS) ^ me) * ROWS + row % ROWS

    row = lax.broadcasted_iota(jnp.int32, (ANC * BLK, BLK), 0)
    slot = (row // PIECE) % ANC
    place = ((row // 8) % QUART) * ROWS + (row // (ANC * PIECE)) * 8 + row % 8
    limit = jnp.where(slot == 0, info_ref[2], info_ref[3])
    bias[0 : ANC * BLK] = jnp.where(place < limit, jnp.float32(0.0), jnp.float32(NEG))
    key_pos = own_pos((BLK, BLK), 0)
    query_pos = own_pos((BLK, BLK), 1)
    bias[ANC * BLK :] = jnp.where(
        (key_pos <= query_pos) & (key_pos < own_len), jnp.float32(0.0), jnp.float32(NEG)
    )


def bias_table(info):
    return pl.pallas_call(
        bias_kernel,
        out_shape=jax.ShapeDtypeStruct((KEYS, BLK), jnp.float32),
        in_specs=[smem()],
        out_specs=whole(1)[0],
        compiler_params=pltpu.CompilerParams(vmem_limit_bytes=8 * MIB),
    )(info)


def attention_kernel(
    head, info_ref, in0, in1, in2, in3, bias, anc_ref, first_ref, out0, out1, far_ref, danc_ref,
    key, val, key_t, val_t, k_acc, v_acc,
):
    ins = (in0, in1, in2, in3)
    outs = ((out0, 0), (out1, 0), (far_ref, 0), (far_ref, PACK))
    base = head * PACK
    me = info_ref[0]
    own_len = info_ref[1]

    def own_pos(shape, dim):
        row = lax.broadcasted_iota(jnp.int32, shape, dim)
        return ((row // ROWS) ^ me) * ROWS + row % ROWS

    live = own_pos((1, BLK), 1) < own_len

    key[0 : ANC * BLK] = anc_ref[head]
    val[0 : ANC * BLK] = anc_ref[PAIR + head]
    for x in range(QUART):
        at = ANC * BLK + x * ROWS
        key[at : at + ROWS] = ins[x][:, base + WIDE : base + WIDE + HEAD_DIM]
        val[at : at + ROWS] = ins[x][:, base + WIDE + HEAD_DIM : base + MAIN]
    key_t[...] = key[...].T
    val_t[...] = val[...].T

    def one(q, g):
        parts = [slice(c, c + CHUNK) for c in range(0, KEYS, CHUNK)]
        scores = [dot(key[c], q, ((1,), (1,))) + bias[c] for c in parts]
        top = functools.reduce(jnp.maximum, [jnp.max(s, axis=0, keepdims=True) for s in scores])
        total = mixed = jnp.float32(0.0)
        es, dps = [], []
        for c, s in zip(parts, scores):
            dp = dot(val[c], g, ((1,), (1,)))
            e = jnp.exp2((s - top) * jnp.float32(SCALE * LOG2E))
            total = total + jnp.sum(e, axis=0, keepdims=True)
            mixed = mixed + jnp.sum(e * dp, axis=0, keepdims=True)
            es.append(e)
            dps.append(dp)
        inv = jnp.float32(1.0) / total
        delta = mixed * inv
        inv = jnp.where(live, inv, jnp.float32(0.0))
        ps = [e * inv for e in es]
        p_b = jnp.concatenate([p.astype(jnp.bfloat16) for p in ps], 0)
        ds = jnp.concatenate([(p * (dp - delta)).astype(jnp.bfloat16) for p, dp in zip(ps, dps)], 0)
        att = dot(val_t[...], p_b, ((1,), (0,)))
        dq = dot(key_t[...], ds, ((1,), (0,))) * jnp.float32(SCALE)
        return p_b, ds, att, dq

    for i in range(GROUP // STEP):
        qs, gs, ps, dss = [], [], [], []
        for j in range(STEP):
            col = (i * STEP + j) * HEAD_DIM
            at = base + col
            q = jnp.concatenate([r[:, at : at + HEAD_DIM] for r in ins], 0)
            at = base + MAIN + col
            g = jnp.concatenate([r[:, at : at + HEAD_DIM] for r in ins], 0)
            p_b, ds, att, dq = one(q, g)
            att = att.T.astype(jnp.bfloat16)
            dq = dq.T.astype(jnp.bfloat16)
            for x in range(QUART):
                out, at = outs[x]
                out[:, at + col : at + col + HEAD_DIM] = att[x * ROWS : (x + 1) * ROWS]
                at = at + MAIN + col
                out[:, at : at + HEAD_DIM] = dq[x * ROWS : (x + 1) * ROWS]
            qs.append(q)
            gs.append(g)
            ps.append(p_b)
            dss.append(ds)
        dk = dot(jnp.concatenate(dss, 1), jnp.concatenate(qs, 0), ((1,), (0,)))
        dv = dot(jnp.concatenate(ps, 1), jnp.concatenate(gs, 0), ((1,), (0,)))
        k_acc[...] = dk if i == 0 else k_acc[...] + dk
        v_acc[...] = dv if i == 0 else v_acc[...] + dv

    k_grad = (k_acc[...] * jnp.float32(SCALE)).astype(jnp.bfloat16)
    v_grad = v_acc[...].astype(jnp.bfloat16)
    if head == 0:
        danc_ref[0] = k_grad[0 : ANC * BLK]
        danc_ref[1] = v_grad[0 : ANC * BLK]
    else:
        danc_ref[0] = first_ref[0]
        danc_ref[1] = k_grad[0 : ANC * BLK]
        danc_ref[2] = first_ref[1]
        danc_ref[3] = v_grad[0 : ANC * BLK]
    for x in range(QUART):
        out, at = outs[x]
        row = ANC * BLK + x * ROWS
        out[:, at + WIDE : at + WIDE + HEAD_DIM] = k_grad[row : row + ROWS]
        out[:, at + WIDE + HEAD_DIM : at + MAIN] = v_grad[row : row + ROWS]


def attention(head, info, packs, bias, anc, first):
    return pl.pallas_call(
        functools.partial(attention_kernel, head),
        out_shape=tuple(jax.ShapeDtypeStruct((ROWS, c), jnp.bfloat16) for c in COLS)
        + (jax.ShapeDtypeStruct((2 * (head + 1), ANC * BLK, HEAD_DIM), jnp.bfloat16),),
        in_specs=[smem()] + whole(QUART + 3),
        out_specs=tuple(whole(len(COLS) + 1)),
        scratch_shapes=[
            pltpu.VMEM((KEYS, HEAD_DIM), jnp.bfloat16),
            pltpu.VMEM((KEYS, HEAD_DIM), jnp.bfloat16),
            pltpu.VMEM((HEAD_DIM, KEYS), jnp.bfloat16),
            pltpu.VMEM((HEAD_DIM, KEYS), jnp.bfloat16),
            pltpu.VMEM((KEYS, HEAD_DIM), jnp.float32),
            pltpu.VMEM((KEYS, HEAD_DIM), jnp.float32),
        ],
        compiler_params=pltpu.CompilerParams(vmem_limit_bytes=32 * MIB),
    )(info, *packs, bias, anc, first)


def pack_kernel(info_ref, q_ref, k_ref, v_ref, g_ref, *outs):
    for x in range(QUART):
        for head in range(PAIR):
            j = (info_ref[0] ^ x) * PAIR + head
            out, base = outs[x], head * PACK
            wide = pl.ds(pl.multiple_of(j * WIDE, WIDE), WIDE)
            narrow = pl.ds(pl.multiple_of(j * HEAD_DIM, HEAD_DIM), HEAD_DIM)
            out[:, base : base + WIDE] = q_ref[:, wide]
            out[:, base + WIDE : base + WIDE + HEAD_DIM] = k_ref[:, narrow]
            out[:, base + WIDE + HEAD_DIM : base + MAIN] = v_ref[:, narrow]
            out[:, base + MAIN : base + PACK] = g_ref[:, wide]


def pack_pieces(info, queries, keys, values, out_grad):
    return pl.pallas_call(
        pack_kernel,
        out_shape=tuple(
            jax.ShapeDtypeStruct((ROWS, PAIR * PACK), jnp.bfloat16) for _ in range(QUART)
        ),
        in_specs=[smem()] + whole(4),
        out_specs=tuple(whole(QUART)),
        compiler_params=pltpu.CompilerParams(vmem_limit_bytes=12 * MIB),
    )(info, queries, keys, values, out_grad)


def place_kernel(info_ref, *refs):
    ins, (att_ref, dq_ref, dkv_ref) = refs[: QUART * PAIR], refs[QUART * PAIR :]
    for x in range(QUART):
        for head in range(PAIR):
            j = (info_ref[0] ^ x) * PAIR + head
            ref = ins[x * PAIR + head]
            wide = pl.ds(pl.multiple_of(j * WIDE, WIDE), WIDE)
            att_ref[:, wide] = ref[:, 0:WIDE]
            dq_ref[:, wide] = ref[:, MAIN:PACK]
            for kv in range(2):
                at = kv * QUART * PAIR * HEAD_DIM + j * HEAD_DIM
                narrow = pl.ds(pl.multiple_of(at, HEAD_DIM), HEAD_DIM)
                col = WIDE + kv * HEAD_DIM
                dkv_ref[:, narrow] = ref[:, col : col + HEAD_DIM]


def place_pieces(info, packs):
    heads = QUART * PAIR
    return pl.pallas_call(
        place_kernel,
        out_shape=(
            jax.ShapeDtypeStruct((ROWS, heads * WIDE), jnp.bfloat16),
            jax.ShapeDtypeStruct((ROWS, heads * WIDE), jnp.bfloat16),
            jax.ShapeDtypeStruct((ROWS, 2 * heads * HEAD_DIM), jnp.bfloat16),
        ),
        in_specs=[smem()] + whole(heads),
        out_specs=tuple(whole(3)),
        compiler_params=pltpu.CompilerParams(vmem_limit_bytes=12 * MIB),
    )(info, *packs)


def partners(x):
    return [(i, i ^ x) for i in range(QUART)]


def body(queries, keys, values, out_grad, ancestors, depths, lengths):
    zh, half, me = lax.axis_index("zh"), lax.axis_index("b"), lax.axis_index("h")
    ctx = (zh * 4 + lax.axis_index("x")) * 4 + lax.axis_index("y")

    tiles = jnp.stack([keys, values]).reshape(2, 4, BLOCKS, 8, QUART, PAIR, HEAD_DIM)
    tiles = jnp.transpose(tiles, (2, 4, 0, 5, 1, 3, 6)).reshape(TP, PLANE * 8, HEAD_DIM)
    tiles = lax.all_to_all(tiles, ("b", "h"), 0, 0, tiled=True)
    tiles = jnp.transpose(tiles.reshape(TP, PLANE, 8, HEAD_DIM), (1, 0, 2, 3))
    tiles = tiles.reshape(PLANE, TP * 8, HEAD_DIM)
    note = ancestors.reshape(1, 1, BLOCKS * ANC).astype(jnp.bfloat16)
    note = jnp.pad(note, ((0, 0), (0, NOTE - 1), (0, HEAD_DIM - BLOCKS * ANC)))
    tiles = jnp.concatenate([tiles, jnp.broadcast_to(note, (PLANE, NOTE, HEAD_DIM))], 1)
    own = lax.all_to_all(tiles, ("x", "y"), 0, 0, tiled=True)
    def swap(x, part):
        return lax.ppermute(part, "h", partners(x)) if x else part

    mine = lax.dynamic_index_in_dim(ancestors, half, 0, keepdims=False)
    depth = lax.dynamic_index_in_dim(depths, half, 0, keepdims=False)
    anc_len = jnp.where(jnp.arange(ANC, dtype=jnp.int32) < depth, lengths[mine], 0)
    own_len = lax.dynamic_index_in_dim(lengths, ctx * BLOCKS + half, 0, keepdims=True)
    info = jnp.concatenate([me.astype(jnp.int32)[None], own_len, anc_len])
    bias = bias_table(info)
    packs = pack_pieces(me.astype(jnp.int32)[None], queries, keys, values, out_grad)
    packs = [swap(x, packs[x]) for x in range(QUART)]

    last = own[PLANE - W + 1 :, : TP * 8].reshape(PREV, PIECE, HEAD_DIM)
    prev = lax.ppermute(last, "zh", [(i, i + 1) for i in range(3)])
    lists = own[:, TP * 8, : BLOCKS * ANC].astype(jnp.int32).reshape(-1)
    idx = jnp.clip(lists - zh * OWN + PREV, 0, PREV + OWN - 1)
    own, *packs[2:] = lax.optimization_barrier((own, *packs[2:]))
    sent = gather_pieces(idx, prev, own).reshape(RELAYS, ANC * PIECE, HEAD_DIM)
    anc = lax.all_to_all(sent, ("x", "y", "b"), 0, 0, tiled=True)
    anc = anc.reshape(2 * PAIR, ANC * BLK, HEAD_DIM)

    own0, near0, far0, danc = attention(0, info, packs, bias, anc, anc)
    own1, near1, far1, danc = attention(1, info, packs, bias, anc, danc)
    far0 = swap(2, far0)
    danc, far0 = lax.optimization_barrier((danc, far0))
    near0, on0 = swap(1, near0), swap(1, far0[:, PACK:])

    danc = danc.reshape(RELAYS, ANC * PIECE, HEAD_DIM)
    terms = lax.all_to_all(danc, ("x", "y", "b"), 0, 0, tiled=True)
    near1, far1 = swap(1, near1), swap(2, far1)
    back, last, total = scatter_pieces(idx, terms.reshape(RELAYS * ANC, PIECE, HEAD_DIM))
    back = lax.ppermute(back, "zh", [(i + 1, i) for i in range(3)])
    back, near0, on0, far1 = lax.optimization_barrier((back, near0, on0, far1))
    on1 = swap(1, far1[:, PACK:])
    last = (last + back.astype(jnp.float32)).astype(jnp.bfloat16)
    total = total.at[OWN - PREV :].set(last).reshape(RELAYS * QUART, 8, HEAD_DIM)
    tiles = lax.all_to_all(total, ("x", "y", "b", "h"), 0, 0, tiled=True)
    tiles = tiles.reshape(2, PAIR, 4, BLOCKS, QUART, 8, HEAD_DIM)
    tiles = jnp.transpose(tiles, (0, 2, 3, 5, 4, 1, 6)).reshape(2, ROWS, QUART * PAIR * HEAD_DIM)

    outs = (own0, own1, near0, near1, far0, far1, on0, on1)
    attended, q_grad, own_grad = place_pieces(info, outs)
    own_grad = own_grad.reshape(ROWS, 2, QUART * PAIR * HEAD_DIM).astype(jnp.float32)
    k_grad = (tiles[0].astype(jnp.float32) + own_grad[:, 0]).astype(jnp.bfloat16)
    v_grad = (tiles[1].astype(jnp.float32) + own_grad[:, 1]).astype(jnp.bfloat16)
    return (attended, q_grad, k_grad, v_grad)


def solution(mesh):
    mesh = Mesh(mesh.devices.reshape(4, 4, 4, BLOCKS, QUART), ("zh", "x", "y", "b", "h"))
    ctx = ("zh", "x", "y")
    rows = P(ctx + ("b", "h"), None)
    in_specs = (rows, rows, rows, rows, P(ctx, None), P(ctx), P())
    return jax.shard_map(
        body, mesh=mesh, in_specs=in_specs, out_specs=(rows,) * 4, check_vma=False
    )
```

```python
import functools

import jax
import jax.numpy as jnp
from jax import lax
from jax.experimental import pallas as pl
from jax.experimental.pallas import tpu as pltpu
from jax.sharding import Mesh
from jax.sharding import PartitionSpec as P

HEAD_DIM = 128
BLK = 256
ANC = 2
W = 4
QUART = 4
GROUP = 8
PAIR = 2
ROWS = BLK // QUART
WIDE = GROUP * HEAD_DIM
MAIN = WIDE + 2 * HEAD_DIM
PACK = MAIN + WIDE
COLS = (PACK, PACK, 2 * PACK)
PACKS = (2 * PACK, 2 * PACK, 2 * PACK, 2 * PACK - WIDE, WIDE)
NOTE = 16
PLANE = 16
BLOCKS = 2
PREV = (W - 1) * BLOCKS
OWN = PLANE * BLOCKS
RELAYS = PLANE * BLOCKS
TP = BLOCKS * QUART
PIECE = BLK // 8
KEYS = ANC * BLK + BLK
CHUNK = 256
STEP = 4
NEG = -1e30
LOG2E = 1.4426950408889634
SCALE = HEAD_DIM ** (-0.5)
MIB = 1024 * 1024


def whole(count):
    return [pl.BlockSpec(memory_space=pltpu.VMEM)] * count


def smem():
    return pl.BlockSpec(memory_space=pltpu.SMEM)


def gather_kernel(idx_ref, prev_ref, own_ref, out_ref, table):
    table[0:PREV] = prev_ref[...]
    for block in range(OWN):
        at = block % BLOCKS * PIECE
        table[PREV + block] = own_ref[block // BLOCKS, at : at + PIECE]
    for entry in range(RELAYS * ANC):
        out_ref[entry] = table[idx_ref[entry]]


def gather_pieces(idx, prev, own):
    return pl.pallas_call(
        gather_kernel,
        out_shape=jax.ShapeDtypeStruct((RELAYS * ANC, PIECE, HEAD_DIM), jnp.bfloat16),
        in_specs=[smem()] + whole(2),
        out_specs=whole(1)[0],
        scratch_shapes=[pltpu.VMEM((PREV + OWN, PIECE, HEAD_DIM), jnp.bfloat16)],
        compiler_params=pltpu.CompilerParams(vmem_limit_bytes=8 * MIB),
    )(idx, prev, own)


def scatter_kernel(idx_ref, terms_ref, prev_ref, last_ref, own_ref, table):
    table[...] = jnp.zeros_like(table)
    for entry in range(RELAYS * ANC):
        place = idx_ref[entry]
        table[place] = table[place] + terms_ref[entry].astype(jnp.float32)
    prev_ref[...] = table[0:PREV].astype(jnp.bfloat16)
    last_ref[...] = table[OWN:]
    own_ref[...] = table[PREV:].astype(jnp.bfloat16)


def scatter_pieces(idx, terms):
    return pl.pallas_call(
        scatter_kernel,
        out_shape=(
            jax.ShapeDtypeStruct((PREV, PIECE, HEAD_DIM), jnp.bfloat16),
            jax.ShapeDtypeStruct((PREV, PIECE, HEAD_DIM), jnp.float32),
            jax.ShapeDtypeStruct((OWN, PIECE, HEAD_DIM), jnp.bfloat16),
        ),
        in_specs=[smem()] + whole(1),
        out_specs=tuple(whole(3)),
        scratch_shapes=[pltpu.VMEM((PREV + OWN, PIECE, HEAD_DIM), jnp.float32)],
        compiler_params=pltpu.CompilerParams(vmem_limit_bytes=8 * MIB),
    )(idx, terms)


def dot(a, b, dims):
    return lax.dot_general(a, b, (dims, ((), ())), preferred_element_type=jnp.float32)


def bias_kernel(info_ref, bias):
    me = info_ref[0]
    own_len = info_ref[1]

    def own_pos(shape, dim):
        row = lax.broadcasted_iota(jnp.int32, shape, dim)
        return ((row // ROWS) ^ me) * ROWS + row % ROWS

    row = lax.broadcasted_iota(jnp.int32, (ANC * BLK, BLK), 0)
    slot = (row // PIECE) % ANC
    place = ((row // 8) % QUART) * ROWS + (row // (ANC * PIECE)) * 8 + row % 8
    limit = jnp.where(slot == 0, info_ref[2], info_ref[3])
    bias[0 : ANC * BLK] = jnp.where(place < limit, jnp.float32(0.0), jnp.float32(NEG))
    key_pos = own_pos((BLK, BLK), 0)
    query_pos = own_pos((BLK, BLK), 1)
    bias[ANC * BLK :] = jnp.where(
        (key_pos <= query_pos) & (key_pos < own_len), jnp.float32(0.0), jnp.float32(NEG)
    )


def bias_table(info):
    return pl.pallas_call(
        bias_kernel,
        out_shape=jax.ShapeDtypeStruct((KEYS, BLK), jnp.float32),
        in_specs=[smem()],
        out_specs=whole(1)[0],
        compiler_params=pltpu.CompilerParams(vmem_limit_bytes=8 * MIB),
    )(info)


def attention_kernel(
    head, info_ref, in0, in1, in2, in3, late, bias, anc_ref, first_ref, out0, out1, far_ref, danc_ref,
    key, val, key_t, val_t, k_acc, v_acc,
):
    ins = (in0, in1, in2, in3)
    outs = ((out0, 0), (out1, 0), (far_ref, 0), (far_ref, PACK))
    base = head * PACK
    grads = [(r, base + MAIN) for r in ins[:-1]] + [(late, 0) if head else (in3, MAIN)]
    me = info_ref[0]
    own_len = info_ref[1]

    def own_pos(shape, dim):
        row = lax.broadcasted_iota(jnp.int32, shape, dim)
        return ((row // ROWS) ^ me) * ROWS + row % ROWS

    live = own_pos((1, BLK), 1) < own_len

    key[0 : ANC * BLK] = anc_ref[head]
    val[0 : ANC * BLK] = anc_ref[PAIR + head]
    for x in range(QUART):
        at = ANC * BLK + x * ROWS
        key[at : at + ROWS] = ins[x][:, base + WIDE : base + WIDE + HEAD_DIM]
        val[at : at + ROWS] = ins[x][:, base + WIDE + HEAD_DIM : base + MAIN]
    key_t[...] = key[...].T
    val_t[...] = val[...].T

    def one(q, g):
        parts = [slice(c, c + CHUNK) for c in range(0, KEYS, CHUNK)]
        scores = [dot(key[c], q, ((1,), (1,))) + bias[c] for c in parts]
        top = functools.reduce(jnp.maximum, [jnp.max(s, axis=0, keepdims=True) for s in scores])
        total = mixed = jnp.float32(0.0)
        es, dps = [], []
        for c, s in zip(parts, scores):
            dp = dot(val[c], g, ((1,), (1,)))
            e = jnp.exp2((s - top) * jnp.float32(SCALE * LOG2E))
            total = total + jnp.sum(e, axis=0, keepdims=True)
            mixed = mixed + jnp.sum(e * dp, axis=0, keepdims=True)
            es.append(e)
            dps.append(dp)
        inv = jnp.float32(1.0) / total
        delta = mixed * inv
        inv = jnp.where(live, inv, jnp.float32(0.0))
        ps = [e * inv for e in es]
        p_b = jnp.concatenate([p.astype(jnp.bfloat16) for p in ps], 0)
        ds = jnp.concatenate([(p * (dp - delta)).astype(jnp.bfloat16) for p, dp in zip(ps, dps)], 0)
        att = dot(val_t[...], p_b, ((1,), (0,)))
        dq = dot(key_t[...], ds, ((1,), (0,))) * jnp.float32(SCALE)
        return p_b, ds, att, dq

    for i in range(GROUP // STEP):
        qs, gs, ps, dss = [], [], [], []
        for j in range(STEP):
            col = (i * STEP + j) * HEAD_DIM
            at = base + col
            q = jnp.concatenate([r[:, at : at + HEAD_DIM] for r in ins], 0)
            ats = [(r, at + col) for r, at in grads]
            g = jnp.concatenate([r[:, at : at + HEAD_DIM] for r, at in ats], 0)
            p_b, ds, att, dq = one(q, g)
            att = att.T.astype(jnp.bfloat16)
            dq = dq.T.astype(jnp.bfloat16)
            for x in range(QUART):
                out, at = outs[x]
                out[:, at + col : at + col + HEAD_DIM] = att[x * ROWS : (x + 1) * ROWS]
                at = at + MAIN + col
                out[:, at : at + HEAD_DIM] = dq[x * ROWS : (x + 1) * ROWS]
            qs.append(q)
            gs.append(g)
            ps.append(p_b)
            dss.append(ds)
        dk = dot(jnp.concatenate(dss, 1), jnp.concatenate(qs, 0), ((1,), (0,)))
        dv = dot(jnp.concatenate(ps, 1), jnp.concatenate(gs, 0), ((1,), (0,)))
        k_acc[...] = dk if i == 0 else k_acc[...] + dk
        v_acc[...] = dv if i == 0 else v_acc[...] + dv

    k_grad = (k_acc[...] * jnp.float32(SCALE)).astype(jnp.bfloat16)
    v_grad = v_acc[...].astype(jnp.bfloat16)
    if head == 0:
        danc_ref[0] = k_grad[0 : ANC * BLK]
        danc_ref[1] = v_grad[0 : ANC * BLK]
    else:
        danc_ref[0] = first_ref[0]
        danc_ref[1] = k_grad[0 : ANC * BLK]
        danc_ref[2] = first_ref[1]
        danc_ref[3] = v_grad[0 : ANC * BLK]
    for x in range(QUART):
        out, at = outs[x]
        row = ANC * BLK + x * ROWS
        out[:, at + WIDE : at + WIDE + HEAD_DIM] = k_grad[row : row + ROWS]
        out[:, at + WIDE + HEAD_DIM : at + MAIN] = v_grad[row : row + ROWS]


def attention(head, info, packs, bias, anc, first):
    return pl.pallas_call(
        functools.partial(attention_kernel, head),
        out_shape=tuple(jax.ShapeDtypeStruct((ROWS, c), jnp.bfloat16) for c in COLS)
        + (jax.ShapeDtypeStruct((2 * (head + 1), ANC * BLK, HEAD_DIM), jnp.bfloat16),),
        in_specs=[smem()] + whole(QUART + 4),
        out_specs=tuple(whole(len(COLS) + 1)),
        scratch_shapes=[
            pltpu.VMEM((KEYS, HEAD_DIM), jnp.bfloat16),
            pltpu.VMEM((KEYS, HEAD_DIM), jnp.bfloat16),
            pltpu.VMEM((HEAD_DIM, KEYS), jnp.bfloat16),
            pltpu.VMEM((HEAD_DIM, KEYS), jnp.bfloat16),
            pltpu.VMEM((KEYS, HEAD_DIM), jnp.float32),
            pltpu.VMEM((KEYS, HEAD_DIM), jnp.float32),
        ],
        compiler_params=pltpu.CompilerParams(vmem_limit_bytes=32 * MIB),
    )(info, *packs, bias, anc, first)


def pack_kernel(info_ref, q_ref, k_ref, v_ref, g_ref, *outs):
    for x in range(QUART):
        for head in range(PAIR):
            j = (info_ref[0] ^ x) * PAIR + head
            out, base = outs[x], head * PACK
            wide = pl.ds(pl.multiple_of(j * WIDE, WIDE), WIDE)
            narrow = pl.ds(pl.multiple_of(j * HEAD_DIM, HEAD_DIM), HEAD_DIM)
            out[:, base : base + WIDE] = q_ref[:, wide]
            out[:, base + WIDE : base + WIDE + HEAD_DIM] = k_ref[:, narrow]
            out[:, base + WIDE + HEAD_DIM : base + MAIN] = v_ref[:, narrow]
            if outs[x].shape[1] >= base + PACK:
                out[:, base + MAIN : base + PACK] = g_ref[:, wide]
            else:
                outs[QUART][...] = g_ref[:, wide]


def pack_pieces(info, queries, keys, values, out_grad):
    return pl.pallas_call(
        pack_kernel,
        out_shape=tuple(
            jax.ShapeDtypeStruct((ROWS, c), jnp.bfloat16) for c in PACKS
        ),
        in_specs=[smem()] + whole(4),
        out_specs=tuple(whole(len(PACKS))),
        compiler_params=pltpu.CompilerParams(vmem_limit_bytes=12 * MIB),
    )(info, queries, keys, values, out_grad)


def place_kernel(info_ref, *refs):
    ins, (att_ref, dq_ref, dkv_ref) = refs[: QUART * PAIR], refs[QUART * PAIR :]
    for x in range(QUART):
        for head in range(PAIR):
            j = (info_ref[0] ^ x) * PAIR + head
            ref = ins[x * PAIR + head]
            wide = pl.ds(pl.multiple_of(j * WIDE, WIDE), WIDE)
            att_ref[:, wide] = ref[:, 0:WIDE]
            dq_ref[:, wide] = ref[:, MAIN:PACK]
            for kv in range(2):
                at = kv * QUART * PAIR * HEAD_DIM + j * HEAD_DIM
                narrow = pl.ds(pl.multiple_of(at, HEAD_DIM), HEAD_DIM)
                col = WIDE + kv * HEAD_DIM
                dkv_ref[:, narrow] = ref[:, col : col + HEAD_DIM]


def place_pieces(info, packs):
    heads = QUART * PAIR
    return pl.pallas_call(
        place_kernel,
        out_shape=(
            jax.ShapeDtypeStruct((ROWS, heads * WIDE), jnp.bfloat16),
            jax.ShapeDtypeStruct((ROWS, heads * WIDE), jnp.bfloat16),
            jax.ShapeDtypeStruct((ROWS, 2 * heads * HEAD_DIM), jnp.bfloat16),
        ),
        in_specs=[smem()] + whole(heads),
        out_specs=tuple(whole(3)),
        compiler_params=pltpu.CompilerParams(vmem_limit_bytes=12 * MIB),
    )(info, *packs)


def partners(x):
    return [(i, i ^ x) for i in range(QUART)]


def body(queries, keys, values, out_grad, ancestors, depths, lengths):
    zh, half, me = lax.axis_index("zh"), lax.axis_index("b"), lax.axis_index("h")
    ctx = (zh * 4 + lax.axis_index("x")) * 4 + lax.axis_index("y")

    tiles = jnp.stack([keys, values]).reshape(2, 4, BLOCKS, 8, QUART, PAIR, HEAD_DIM)
    tiles = jnp.transpose(tiles, (2, 4, 0, 5, 1, 3, 6)).reshape(TP, PLANE * 8, HEAD_DIM)
    tiles = lax.all_to_all(tiles, ("b", "h"), 0, 0, tiled=True)
    tiles = jnp.transpose(tiles.reshape(TP, PLANE, 8, HEAD_DIM), (1, 0, 2, 3))
    tiles = tiles.reshape(PLANE, TP * 8, HEAD_DIM)
    note = ancestors.reshape(1, 1, BLOCKS * ANC).astype(jnp.bfloat16)
    note = jnp.pad(note, ((0, 0), (0, NOTE - 1), (0, HEAD_DIM - BLOCKS * ANC)))
    tiles = jnp.concatenate([tiles, jnp.broadcast_to(note, (PLANE, NOTE, HEAD_DIM))], 1)
    own = lax.all_to_all(tiles, ("x", "y"), 0, 0, tiled=True)
    def swap(x, part):
        return lax.ppermute(part, "h", partners(x)) if x else part

    mine = lax.dynamic_index_in_dim(ancestors, half, 0, keepdims=False)
    depth = lax.dynamic_index_in_dim(depths, half, 0, keepdims=False)
    anc_len = jnp.where(jnp.arange(ANC, dtype=jnp.int32) < depth, lengths[mine], 0)
    own_len = lax.dynamic_index_in_dim(lengths, ctx * BLOCKS + half, 0, keepdims=True)
    info = jnp.concatenate([me.astype(jnp.int32)[None], own_len, anc_len])
    bias = bias_table(info)
    packs = pack_pieces(me.astype(jnp.int32)[None], queries, keys, values, out_grad)
    packs = [swap(x, part) for x, part in zip((0, 1, 2, 3, 3), packs)]

    last = own[PLANE - W + 1 :, : TP * 8].reshape(PREV, PIECE, HEAD_DIM)
    prev = lax.ppermute(last, "zh", [(i, i + 1) for i in range(3)])
    lists = own[:, TP * 8, : BLOCKS * ANC].astype(jnp.int32).reshape(-1)
    idx = jnp.clip(lists - zh * OWN + PREV, 0, PREV + OWN - 1)
    own, *packs[1:4] = lax.optimization_barrier((own, *packs[1:4]))
    sent = gather_pieces(idx, prev, own).reshape(RELAYS, ANC * PIECE, HEAD_DIM)
    anc = lax.all_to_all(sent, ("x", "y", "b"), 0, 0, tiled=True)
    anc, packs[4] = lax.optimization_barrier((anc, packs[4]))
    anc = anc.reshape(2 * PAIR, ANC * BLK, HEAD_DIM)

    own0, near0, far0, danc = attention(0, info, packs, bias, anc, anc)
    own1, near1, far1, danc = attention(1, info, packs, bias, anc, danc)
    far0 = swap(2, far0)
    danc, far0 = lax.optimization_barrier((danc, far0))
    near0, on0 = swap(1, near0), swap(1, far0[:, PACK:])

    danc = danc.reshape(RELAYS, ANC * PIECE, HEAD_DIM)
    terms = lax.all_to_all(danc, ("x", "y", "b"), 0, 0, tiled=True)
    near1, far1 = swap(1, near1), swap(2, far1)
    back, last, total = scatter_pieces(idx, terms.reshape(RELAYS * ANC, PIECE, HEAD_DIM))
    back = lax.ppermute(back, "zh", [(i + 1, i) for i in range(3)])
    back, near0, on0, far1 = lax.optimization_barrier((back, near0, on0, far1))
    on1 = swap(1, far1[:, PACK:])
    last = (last + back.astype(jnp.float32)).astype(jnp.bfloat16)
    total = total.at[OWN - PREV :].set(last).reshape(RELAYS * QUART, 8, HEAD_DIM)
    tiles = lax.all_to_all(total, ("x", "y", "b", "h"), 0, 0, tiled=True)
    tiles = tiles.reshape(2, PAIR, 4, BLOCKS, QUART, 8, HEAD_DIM)
    tiles = jnp.transpose(tiles, (0, 2, 3, 5, 4, 1, 6)).reshape(2, ROWS, QUART * PAIR * HEAD_DIM)

    outs = (own0, own1, near0, near1, far0, far1, on0, on1)
    attended, q_grad, own_grad = place_pieces(info, outs)
    own_grad = own_grad.reshape(ROWS, 2, QUART * PAIR * HEAD_DIM).astype(jnp.float32)
    k_grad = (tiles[0].astype(jnp.float32) + own_grad[:, 0]).astype(jnp.bfloat16)
    v_grad = (tiles[1].astype(jnp.float32) + own_grad[:, 1]).astype(jnp.bfloat16)
    return (attended, q_grad, k_grad, v_grad)


def solution(mesh):
    mesh = Mesh(mesh.devices.reshape(4, 4, 4, BLOCKS, QUART), ("zh", "x", "y", "b", "h"))
    ctx = ("zh", "x", "y")
    rows = P(ctx + ("b", "h"), None)
    in_specs = (rows, rows, rows, rows, P(ctx, None), P(ctx), P())
    return jax.shard_map(
        body, mesh=mesh, in_specs=in_specs, out_specs=(rows,) * 4, check_vma=False
    )
```

```python
import functools

import jax
import jax.numpy as jnp
from jax import lax
from jax.experimental import pallas as pl
from jax.experimental.pallas import tpu as pltpu
from jax.sharding import Mesh
from jax.sharding import PartitionSpec as P

HEAD_DIM = 128
BLK = 256
ANC = 2
W = 4
QUART = 4
GROUP = 8
PAIR = 2
ROWS = BLK // QUART
WIDE = GROUP * HEAD_DIM
MAIN = WIDE + 2 * HEAD_DIM
PACK = MAIN + WIDE
COLS = (PACK, PACK, 2 * PACK)
PACKS = (2 * PACK, 2 * PACK, 2 * PACK, 2 * PACK - WIDE, WIDE)
NOTE = 16
PLANE = 16
BLOCKS = 2
PREV = (W - 1) * BLOCKS
OWN = PLANE * BLOCKS
RELAYS = PLANE * BLOCKS
TP = BLOCKS * QUART
PIECE = BLK // 8
KEYS = ANC * BLK + BLK
CHUNK = 256
STEP = 4
NEG = -1e30
LOG2E = 1.4426950408889634
SCALE = HEAD_DIM ** (-0.5)
MIB = 1024 * 1024


def whole(count):
    return [pl.BlockSpec(memory_space=pltpu.VMEM)] * count


def smem():
    return pl.BlockSpec(memory_space=pltpu.SMEM)


def gather_kernel(idx_ref, prev_ref, own_ref, out_ref, table):
    table[0:PREV] = prev_ref[...]
    for block in range(OWN):
        at = block % BLOCKS * PIECE
        table[PREV + block] = own_ref[block // BLOCKS, at : at + PIECE]
    for entry in range(RELAYS * ANC):
        out_ref[entry] = table[idx_ref[entry]]


def gather_pieces(idx, prev, own):
    return pl.pallas_call(
        gather_kernel,
        out_shape=jax.ShapeDtypeStruct((RELAYS * ANC, PIECE, HEAD_DIM), jnp.bfloat16),
        in_specs=[smem()] + whole(2),
        out_specs=whole(1)[0],
        scratch_shapes=[pltpu.VMEM((PREV + OWN, PIECE, HEAD_DIM), jnp.bfloat16)],
        compiler_params=pltpu.CompilerParams(vmem_limit_bytes=8 * MIB),
    )(idx, prev, own)


def scatter_kernel(idx_ref, terms_ref, prev_ref, last_ref, own_ref, table):
    table[...] = jnp.zeros_like(table)
    for entry in range(RELAYS * ANC):
        place = idx_ref[entry]
        table[place] = table[place] + terms_ref[entry].astype(jnp.float32)
    prev_ref[...] = table[0:PREV].astype(jnp.bfloat16)
    last_ref[...] = table[OWN:]
    own_ref[...] = table[PREV:].astype(jnp.bfloat16)


def scatter_pieces(idx, terms):
    return pl.pallas_call(
        scatter_kernel,
        out_shape=(
            jax.ShapeDtypeStruct((PREV, PIECE, HEAD_DIM), jnp.bfloat16),
            jax.ShapeDtypeStruct((PREV, PIECE, HEAD_DIM), jnp.float32),
            jax.ShapeDtypeStruct((OWN, PIECE, HEAD_DIM), jnp.bfloat16),
        ),
        in_specs=[smem()] + whole(1),
        out_specs=tuple(whole(3)),
        scratch_shapes=[pltpu.VMEM((PREV + OWN, PIECE, HEAD_DIM), jnp.float32)],
        compiler_params=pltpu.CompilerParams(vmem_limit_bytes=8 * MIB),
    )(idx, terms)


def dot(a, b, dims):
    return lax.dot_general(a, b, (dims, ((), ())), preferred_element_type=jnp.float32)


def bias_kernel(info_ref, bias):
    me = info_ref[0]
    own_len = info_ref[1]

    def own_pos(shape, dim):
        row = lax.broadcasted_iota(jnp.int32, shape, dim)
        return ((row // ROWS) ^ me) * ROWS + row % ROWS

    row = lax.broadcasted_iota(jnp.int32, (ANC * BLK, BLK), 0)
    slot = (row // PIECE) % ANC
    place = ((row // 8) % QUART) * ROWS + (row // (ANC * PIECE)) * 8 + row % 8
    limit = jnp.where(slot == 0, info_ref[2], info_ref[3])
    bias[0 : ANC * BLK] = jnp.where(place < limit, jnp.float32(0.0), jnp.float32(NEG))
    key_pos = own_pos((BLK, BLK), 0)
    query_pos = own_pos((BLK, BLK), 1)
    bias[ANC * BLK :] = jnp.where(
        (key_pos <= query_pos) & (key_pos < own_len), jnp.float32(0.0), jnp.float32(NEG)
    )


def bias_table(info):
    return pl.pallas_call(
        bias_kernel,
        out_shape=jax.ShapeDtypeStruct((KEYS, BLK), jnp.float32),
        in_specs=[smem()],
        out_specs=whole(1)[0],
        compiler_params=pltpu.CompilerParams(vmem_limit_bytes=8 * MIB),
    )(info)


def attention_kernel(
    head, info_ref, in0, in1, in2, in3, late, bias, anc_ref, first_ref, out0, out1, far_ref, danc_ref,
    key, val, key_t, val_t, k_acc, v_acc,
):
    ins = (in0, in1, in2, in3)
    outs = ((out0, 0), (out1, 0), (far_ref, 0), (far_ref, PACK))
    base = head * PACK
    grads = [(r, base + MAIN) for r in ins[:-1]] + [(late, 0) if head else (in3, MAIN)]
    me = info_ref[0]
    own_len = info_ref[1]

    def own_pos(shape, dim):
        row = lax.broadcasted_iota(jnp.int32, shape, dim)
        return ((row // ROWS) ^ me) * ROWS + row % ROWS

    live = own_pos((1, BLK), 1) < own_len

    key[0 : ANC * BLK] = anc_ref[head]
    val[0 : ANC * BLK] = anc_ref[PAIR + head]
    for x in range(QUART):
        at = ANC * BLK + x * ROWS
        key[at : at + ROWS] = ins[x][:, base + WIDE : base + WIDE + HEAD_DIM]
        val[at : at + ROWS] = ins[x][:, base + WIDE + HEAD_DIM : base + MAIN]
    key_t[...] = key[...].T
    val_t[...] = val[...].T

    def one(q, g):
        parts = [slice(c, c + CHUNK) for c in range(0, KEYS, CHUNK)]
        scores = [dot(key[c], q, ((1,), (1,))) + bias[c] for c in parts]
        top = functools.reduce(jnp.maximum, [jnp.max(s, axis=0, keepdims=True) for s in scores])
        total = mixed = jnp.float32(0.0)
        es, dps = [], []
        for c, s in zip(parts, scores):
            dp = dot(val[c], g, ((1,), (1,)))
            e = jnp.exp2((s - top) * jnp.float32(SCALE * LOG2E))
            total = total + jnp.sum(e, axis=0, keepdims=True)
            mixed = mixed + jnp.sum(e * dp, axis=0, keepdims=True)
            es.append(e)
            dps.append(dp)
        inv = jnp.float32(1.0) / total
        delta = mixed * inv
        inv = jnp.where(live, inv, jnp.float32(0.0))
        ps = [e * inv for e in es]
        p_b = jnp.concatenate([p.astype(jnp.bfloat16) for p in ps], 0)
        ds = jnp.concatenate([(p * (dp - delta)).astype(jnp.bfloat16) for p, dp in zip(ps, dps)], 0)
        att = dot(val_t[...], p_b, ((1,), (0,)))
        dq = dot(key_t[...], ds, ((1,), (0,))) * jnp.float32(SCALE)
        return p_b, ds, att, dq

    for i in range(GROUP // STEP):
        qs, gs, ps, dss = [], [], [], []
        for j in range(STEP):
            col = (i * STEP + j) * HEAD_DIM
            at = base + col
            q = jnp.concatenate([r[:, at : at + HEAD_DIM] for r in ins], 0)
            ats = [(r, at + col) for r, at in grads]
            g = jnp.concatenate([r[:, at : at + HEAD_DIM] for r, at in ats], 0)
            p_b, ds, att, dq = one(q, g)
            att = att.T.astype(jnp.bfloat16)
            dq = dq.T.astype(jnp.bfloat16)
            for x in range(QUART):
                out, at = outs[x]
                out[:, at + col : at + col + HEAD_DIM] = att[x * ROWS : (x + 1) * ROWS]
                at = at + MAIN + col
                out[:, at : at + HEAD_DIM] = dq[x * ROWS : (x + 1) * ROWS]
            qs.append(q)
            gs.append(g)
            ps.append(p_b)
            dss.append(ds)
        dk = dot(jnp.concatenate(dss, 1), jnp.concatenate(qs, 0), ((1,), (0,)))
        dv = dot(jnp.concatenate(ps, 1), jnp.concatenate(gs, 0), ((1,), (0,)))
        k_acc[...] = dk if i == 0 else k_acc[...] + dk
        v_acc[...] = dv if i == 0 else v_acc[...] + dv

    k_grad = (k_acc[...] * jnp.float32(SCALE)).astype(jnp.bfloat16)
    v_grad = v_acc[...].astype(jnp.bfloat16)
    if head == 0:
        danc_ref[0] = k_grad[0 : ANC * BLK]
        danc_ref[1] = v_grad[0 : ANC * BLK]
    else:
        danc_ref[0] = first_ref[0]
        danc_ref[1] = k_grad[0 : ANC * BLK]
        danc_ref[2] = first_ref[1]
        danc_ref[3] = v_grad[0 : ANC * BLK]
    for x in range(QUART):
        out, at = outs[x]
        row = ANC * BLK + x * ROWS
        out[:, at + WIDE : at + WIDE + HEAD_DIM] = k_grad[row : row + ROWS]
        out[:, at + WIDE + HEAD_DIM : at + MAIN] = v_grad[row : row + ROWS]


def attention(head, info, packs, bias, anc, first):
    return pl.pallas_call(
        functools.partial(attention_kernel, head),
        out_shape=tuple(jax.ShapeDtypeStruct((ROWS, c), jnp.bfloat16) for c in COLS)
        + (jax.ShapeDtypeStruct((2 * (head + 1), ANC * BLK, HEAD_DIM), jnp.bfloat16),),
        in_specs=[smem()] + whole(QUART + 4),
        out_specs=tuple(whole(len(COLS) + 1)),
        scratch_shapes=[
            pltpu.VMEM((KEYS, HEAD_DIM), jnp.bfloat16),
            pltpu.VMEM((KEYS, HEAD_DIM), jnp.bfloat16),
            pltpu.VMEM((HEAD_DIM, KEYS), jnp.bfloat16),
            pltpu.VMEM((HEAD_DIM, KEYS), jnp.bfloat16),
            pltpu.VMEM((KEYS, HEAD_DIM), jnp.float32),
            pltpu.VMEM((KEYS, HEAD_DIM), jnp.float32),
        ],
        compiler_params=pltpu.CompilerParams(vmem_limit_bytes=32 * MIB),
    )(info, *packs, bias, anc, first)


def pack_kernel(info_ref, q_ref, k_ref, v_ref, g_ref, *outs):
    for x in range(QUART):
        for head in range(PAIR):
            j = (info_ref[0] ^ x) * PAIR + head
            out, base = outs[x], head * PACK
            wide = pl.ds(pl.multiple_of(j * WIDE, WIDE), WIDE)
            narrow = pl.ds(pl.multiple_of(j * HEAD_DIM, HEAD_DIM), HEAD_DIM)
            out[:, base : base + WIDE] = q_ref[:, wide]
            out[:, base + WIDE : base + WIDE + HEAD_DIM] = k_ref[:, narrow]
            out[:, base + WIDE + HEAD_DIM : base + MAIN] = v_ref[:, narrow]
            if outs[x].shape[1] >= base + PACK:
                out[:, base + MAIN : base + PACK] = g_ref[:, wide]
            else:
                outs[QUART][...] = g_ref[:, wide]


def pack_pieces(info, queries, keys, values, out_grad):
    return pl.pallas_call(
        pack_kernel,
        out_shape=tuple(
            jax.ShapeDtypeStruct((ROWS, c), jnp.bfloat16) for c in PACKS
        ),
        in_specs=[smem()] + whole(4),
        out_specs=tuple(whole(len(PACKS))),
        compiler_params=pltpu.CompilerParams(vmem_limit_bytes=12 * MIB),
    )(info, queries, keys, values, out_grad)


def place_kernel(info_ref, *refs):
    ins, (att_ref, dq_ref, dkv_ref) = refs[: QUART * PAIR], refs[QUART * PAIR :]
    for x in range(QUART):
        for head in range(PAIR):
            j = (info_ref[0] ^ x) * PAIR + head
            ref = ins[x * PAIR + head]
            wide = pl.ds(pl.multiple_of(j * WIDE, WIDE), WIDE)
            att_ref[:, wide] = ref[:, 0:WIDE]
            dq_ref[:, wide] = ref[:, MAIN:PACK]
            for kv in range(2):
                at = kv * QUART * PAIR * HEAD_DIM + j * HEAD_DIM
                narrow = pl.ds(pl.multiple_of(at, HEAD_DIM), HEAD_DIM)
                col = WIDE + kv * HEAD_DIM
                dkv_ref[:, narrow] = ref[:, col : col + HEAD_DIM]


def place_pieces(info, packs):
    heads = QUART * PAIR
    return pl.pallas_call(
        place_kernel,
        out_shape=(
            jax.ShapeDtypeStruct((ROWS, heads * WIDE), jnp.bfloat16),
            jax.ShapeDtypeStruct((ROWS, heads * WIDE), jnp.bfloat16),
            jax.ShapeDtypeStruct((ROWS, 2 * heads * HEAD_DIM), jnp.bfloat16),
        ),
        in_specs=[smem()] + whole(heads),
        out_specs=tuple(whole(3)),
        compiler_params=pltpu.CompilerParams(vmem_limit_bytes=12 * MIB),
    )(info, *packs)


def partners(x):
    return [(i, i ^ x) for i in range(QUART)]


def body(queries, keys, values, out_grad, ancestors, depths, lengths):
    zh, half, me = lax.axis_index("zh"), lax.axis_index("b"), lax.axis_index("h")
    ctx = (zh * 4 + lax.axis_index("x")) * 4 + lax.axis_index("y")

    def tiles_of(a):
        a = a.reshape(4, BLOCKS, 8, QUART, PAIR, HEAD_DIM)
        return jnp.transpose(a, (1, 3, 4, 0, 2, 5)).reshape(TP, PLANE * 4, HEAD_DIM)

    tiles = jnp.concatenate([tiles_of(keys), tiles_of(values)], 1)
    tiles = lax.all_to_all(tiles, ("b", "h"), 0, 0, tiled=True)
    tiles = jnp.transpose(tiles.reshape(TP, PLANE, 8, HEAD_DIM), (1, 0, 2, 3))
    tiles = tiles.reshape(PLANE, TP * 8, HEAD_DIM)
    note = ancestors.reshape(1, 1, BLOCKS * ANC).astype(jnp.bfloat16)
    note = jnp.pad(note, ((0, 0), (0, NOTE - 1), (0, HEAD_DIM - BLOCKS * ANC)))
    tiles = jnp.concatenate([tiles, jnp.broadcast_to(note, (PLANE, NOTE, HEAD_DIM))], 1)
    own = lax.all_to_all(tiles, ("x", "y"), 0, 0, tiled=True)
    def swap(x, part):
        return lax.ppermute(part, "h", partners(x)) if x else part

    mine = lax.dynamic_index_in_dim(ancestors, half, 0, keepdims=False)
    depth = lax.dynamic_index_in_dim(depths, half, 0, keepdims=False)
    anc_len = jnp.where(jnp.arange(ANC, dtype=jnp.int32) < depth, lengths[mine], 0)
    own_len = lax.dynamic_index_in_dim(lengths, ctx * BLOCKS + half, 0, keepdims=True)
    info = jnp.concatenate([me.astype(jnp.int32)[None], own_len, anc_len])
    bias = bias_table(info)
    packs = pack_pieces(me.astype(jnp.int32)[None], queries, keys, values, out_grad)
    packs = [swap(x, part) for x, part in zip((0, 1, 2, 3, 3), packs)]

    last = own[PLANE - W + 1 :, : TP * 8].reshape(PREV, PIECE, HEAD_DIM)
    prev = lax.ppermute(last, "zh", [(i, i + 1) for i in range(3)])
    lists = own[:, TP * 8, : BLOCKS * ANC].astype(jnp.int32).reshape(-1)
    idx = jnp.clip(lists - zh * OWN + PREV, 0, PREV + OWN - 1)
    own, *packs[1:4] = lax.optimization_barrier((own, *packs[1:4]))
    sent = gather_pieces(idx, prev, own).reshape(RELAYS, ANC * PIECE, HEAD_DIM)
    anc = lax.all_to_all(sent, ("x", "y", "b"), 0, 0, tiled=True)
    anc, packs[4] = lax.optimization_barrier((anc, packs[4]))
    anc = anc.reshape(2 * PAIR, ANC * BLK, HEAD_DIM)

    own0, near0, far0, danc = attention(0, info, packs, bias, anc, anc)
    own1, near1, far1, danc = attention(1, info, packs, bias, anc, danc)
    far0 = swap(2, far0)
    danc, far0 = lax.optimization_barrier((danc, far0))
    near0, on0 = swap(1, near0), swap(1, far0[:, PACK:])

    danc = danc.reshape(RELAYS, ANC * PIECE, HEAD_DIM)
    terms = lax.all_to_all(danc, ("x", "y", "b"), 0, 0, tiled=True)
    near1, far1 = swap(1, near1), swap(2, far1)
    back, last, total = scatter_pieces(idx, terms.reshape(RELAYS * ANC, PIECE, HEAD_DIM))
    back = lax.ppermute(back, "zh", [(i + 1, i) for i in range(3)])
    back, near0, on0, far1 = lax.optimization_barrier((back, near0, on0, far1))
    on1 = swap(1, far1[:, PACK:])
    last = (last + back.astype(jnp.float32)).astype(jnp.bfloat16)
    total = total.at[OWN - PREV :].set(last).reshape(RELAYS * QUART, 8, HEAD_DIM)
    tiles = lax.all_to_all(total, ("x", "y", "b", "h"), 0, 0, tiled=True)
    tiles = tiles.reshape(2, PAIR, 4, BLOCKS, QUART, 8, HEAD_DIM)
    tiles = jnp.transpose(tiles, (0, 2, 3, 5, 4, 1, 6)).reshape(2, ROWS, QUART * PAIR * HEAD_DIM)

    outs = (own0, own1, near0, near1, far0, far1, on0, on1)
    attended, q_grad, own_grad = place_pieces(info, outs)
    own_grad = own_grad.reshape(ROWS, 2, QUART * PAIR * HEAD_DIM).astype(jnp.float32)
    k_grad = (tiles[0].astype(jnp.float32) + own_grad[:, 0]).astype(jnp.bfloat16)
    v_grad = (tiles[1].astype(jnp.float32) + own_grad[:, 1]).astype(jnp.bfloat16)
    return (attended, q_grad, k_grad, v_grad)


def solution(mesh):
    mesh = Mesh(mesh.devices.reshape(4, 4, 4, BLOCKS, QUART), ("zh", "x", "y", "b", "h"))
    ctx = ("zh", "x", "y")
    rows = P(ctx + ("b", "h"), None)
    in_specs = (rows, rows, rows, rows, P(ctx, None), P(ctx), P())
    return jax.shard_map(
        body, mesh=mesh, in_specs=in_specs, out_specs=(rows,) * 4, check_vma=False
    )
```
